256 devices in a mesh: req: 16 (over x, z_lo), patch: 16 (over z_hi, y, core).
Axes of the slice: x: 4, y: 4, z: 8 (z_hi: 2, z_lo: 4; z = z_hi * 4 + z_lo), core: 2. Of those that a mesh axis runs over, the one named last changes fastest.
Arguments:
- tokens: bfloat16 [16, 2048, 3072], P('req', 'patch'), may hold values from -28 to 28, as said below
- projection_weight: bfloat16 [3072, 16, 384], P(None, 'patch'), may hold values from -0.109375 to 0.109375
- projection_bias: bfloat16 [16, 384], P('patch'), may hold values from -3 to 3
- adapter_down_weight: bfloat16 [16, 3072, 32], P('req'), may hold values from -0.109375 to 0.109375
- adapter_up_weight: bfloat16 [16, 32, 16, 384], P('req', None, 'patch'), may hold values from -1 to 1
- tile_allow_mask: int32 [16, 16, 32], P('req'), may hold values 0 or 1
- references: int32 [4], replicated, may hold values from 0 to 15, as said below
- pairing: int32 [16], replicated, may hold values from 0 to 3
Outputs:
- mixed: bfloat16 [16, 2048, 2048], P('req', 'patch')
The draws below stay inside these ranges and needn't reach their ends.
Inputs may be any that keep to these rules, and one draw needn't show every extreme that they name: Draws of tokens stay in this range. `references`: 4 distinct request indices; the last request is always one of them.
All inputs are finite; a program needn't handle non-finite values. No bound on the sum of `tile_allow_mask` on one device may be relied on, other than what follows from the above.
Results may differ from the reference program's by a relative error of at most 0.04.
Values may be sent and summed in bfloat16 or wider, within the bound.
A program may use at most 64 MiB of HBM per device.

```python
import math
import jax
import jax.numpy as jnp
import numpy as np
from jax import lax

MODEL_WIDTH = 3072
HEAD_DIMENSION = 128
LOCAL_HEADS = 16
ADAPTER_RANK = 32
TILE = 128
NREF = 4
REQUEST_COUNT = 16
SEQ = 2048
TILES = 16


def draw_tokens(key, part):
    values = jnp.clip(jax.random.normal(key, (REQUEST_COUNT, SEQ, MODEL_WIDTH), jnp.float32), -6.0, 6.0)
    return values.astype(jnp.bfloat16)


def draw_references(key, part):
    key = jax.random.fold_in(key, 7)
    first_key, second_key = jax.random.split(key)
    others = jax.random.permutation(first_key, REQUEST_COUNT - 1)[:NREF - 1].astype(jnp.int32)
    chosen = jnp.concatenate([others, jnp.full((1,), REQUEST_COUNT - 1, jnp.int32)], 0)
    return jax.random.permutation(second_key, chosen).astype(jnp.int32)


def plant(entries, rng, least, largest):
    longest = entries.shape.index(max(entries.shape))
    spots = []
    for shift in (0, 1):
        where = [jax.random.randint(jax.random.fold_in(rng, axis), (), 0, length) for axis, length in enumerate(entries.shape)]
        where[longest] = (where[longest] + shift) % entries.shape[longest]
        spots.append(tuple(where))
    return entries.at[spots[0]].set(least).at[spots[1]].set(largest)


def levels(stream_key, dims, cuts, smallest, high):
    level, own = 1.0, jax.random.fold_in(stream_key, 6)
    for axis_at, parts in cuts:
        steps = jnp.exp(jax.random.uniform(jax.random.fold_in(own, axis_at), (parts,), jnp.float32, smallest / len(cuts), high / len(cuts)))
        level = level * jnp.repeat(steps, dims[axis_at] // parts).reshape([-1 if axis == axis_at else 1 for axis in range(len(dims))])
    return level


def cumulative_ranks(amount, skew):
    portions = [(1 << 20) // math.isqrt(rank ** skew) + 1 for rank in range(1, amount + 1)]
    deviation = 1 + sum(portions) // (1 << 30)
    return np.cumsum(np.array([max(1, weight // deviation) for weight in portions]))


def ranked(key, dims, amount, slope):
    listing = cumulative_ranks(amount, slope)
    ticket = jax.random.randint(jax.random.fold_in(key, 1), dims, 0, int(listing[amount - 1]))
    rank = jnp.searchsorted(jnp.asarray(listing, jnp.int32), ticket, side="right")
    return jax.random.permutation(jax.random.fold_in(key, 2), amount)[rank].astype(jnp.int32)


def bell_draw(own_key, shape, deviation, most, cuts=(), kind=jnp.bfloat16):
    entries = deviation * jax.random.normal(own_key, shape, jnp.float32)
    if cuts:
        entries = entries * levels(own_key, shape, cuts, -0.22, 0.18)
    return jnp.clip(entries, -most, most).astype(kind)


def setup_inputs(seed: int = 0) -> dict:
    seeds = jax.random.split(jax.random.key(seed), 9)
    tokens = draw_tokens(jax.random.fold_in(seeds[8], 71), 0)
    projection_weight = bell_draw(seeds[1], (MODEL_WIDTH, LOCAL_HEADS, 3 * HEAD_DIMENSION), MODEL_WIDTH ** -0.5, 0.109375, ((1, 16),))
    projection_bias = bell_draw(seeds[2], (LOCAL_HEADS, 3 * HEAD_DIMENSION), 0.5, 3.0, ((0, 16),))
    adapter_down_weight = bell_draw(seeds[3], (REQUEST_COUNT, MODEL_WIDTH, ADAPTER_RANK), MODEL_WIDTH ** -0.5, 0.109375, ((0, 16),))
    adapter_up_weight = bell_draw(seeds[4], (REQUEST_COUNT, ADAPTER_RANK, LOCAL_HEADS, 3 * HEAD_DIMENSION), ADAPTER_RANK ** -0.5, 1.0, ((0, 16), (2, 16)))
    tile_allow_mask = plant((jax.random.randint(seeds[5], (REQUEST_COUNT, TILES, 2 * TILES), 0, 2) < 1).astype(jnp.int32), jax.random.fold_in(seeds[5], 1), 0, 1)
    references = draw_references(jax.random.fold_in(seeds[8], 71), 0)
    pairing = plant(ranked(seeds[7], (REQUEST_COUNT,), NREF, 2), jax.random.fold_in(seeds[7], 3), 0, NREF - 1).astype(jnp.int32)
    return dict(tokens=tokens, projection_weight=projection_weight, projection_bias=projection_bias, adapter_down_weight=adapter_down_weight, adapter_up_weight=adapter_up_weight, tile_allow_mask=tile_allow_mask, references=references, pairing=pairing)


def apply_projection(inputs, projection_weight, projection_bias):
    token_rows, down_req, up_req = inputs
    rows_f32 = token_rows.astype(jnp.float32)
    lowrank = jnp.dot(rows_f32, down_req.astype(jnp.float32)).astype(jnp.bfloat16)
    lowrank = lax.optimization_barrier(lowrank).astype(jnp.float32)
    base_part = jnp.einsum("td,dhe->the", rows_f32, projection_weight.astype(jnp.float32))
    lowrank_part = jnp.einsum("tr,rhe->the", lowrank, up_req.astype(jnp.float32))
    return (base_part + lowrank_part + projection_bias.astype(jnp.float32)).astype(jnp.bfloat16)


def reference(tokens, projection_weight, projection_bias, adapter_down_weight, adapter_up_weight, tile_allow_mask, references, pairing):
    projected_rows = lax.map(lambda request_entry: apply_projection(request_entry, projection_weight, projection_bias), (tokens, adapter_down_weight, adapter_up_weight))
    block_rows = min(512, SEQ)
    score_scale = HEAD_DIMENSION ** -0.5
    rows_tile = jnp.arange(TILES, dtype=jnp.int32)
    cols_tile = jnp.arange(2 * TILES, dtype=jnp.int32)

    def request(request_index):
        mine = lax.dynamic_index_in_dim(projected_rows, request_index, 0, keepdims=False)
        slot_index = lax.dynamic_index_in_dim(pairing, request_index, 0, keepdims=False)
        owner_index = lax.dynamic_index_in_dim(references, slot_index, 0, keepdims=False)
        theirs = lax.dynamic_index_in_dim(projected_rows, owner_index, 0, keepdims=False)
        key_pairs = jnp.concatenate([mine[..., HEAD_DIMENSION:], theirs[..., HEAD_DIMENSION:]], 0).astype(jnp.float32)
        own_mask = lax.dynamic_index_in_dim(tile_allow_mask, request_index, 0, keepdims=False)
        tile_allow = (own_mask == 1) | (rows_tile[:, None] == cols_tile[None, :])
        wide_allow = jnp.repeat(tile_allow, TILE, axis=1)
        queries = mine[..., :HEAD_DIMENSION].astype(jnp.float32)

        def one_block(block_index):
            first_row = block_index * block_rows
            row_allow = jnp.repeat(lax.dynamic_slice_in_dim(wide_allow, first_row // TILE, block_rows // TILE, 0), TILE, axis=0)
            query_block = lax.dynamic_slice_in_dim(queries, first_row, block_rows, 0)
            scores = jnp.einsum("qhd,khd->hqk", query_block, key_pairs[..., :HEAD_DIMENSION]) * score_scale
            scores = jnp.where(row_allow[None], scores, -jnp.inf)
            row_max = jnp.max(scores, axis=-1, keepdims=True)
            weights = jnp.exp(scores - row_max)
            row_total = jnp.sum(weights, axis=-1, keepdims=True)
            probability = (weights / row_total).astype(jnp.bfloat16)
            probability = lax.optimization_barrier(probability).astype(jnp.float32)
            result = jnp.einsum("hqk,khd->qhd", probability, key_pairs[..., HEAD_DIMENSION:])
            return result.astype(jnp.bfloat16)

        blocks_out = lax.map(one_block, jnp.arange(SEQ // block_rows, dtype=jnp.int32))
        return blocks_out.reshape(SEQ, LOCAL_HEADS * HEAD_DIMENSION)

    return lax.map(request, jnp.arange(REQUEST_COUNT, dtype=jnp.int32))
```

```python
import functools, math
import jax, jax.numpy as jnp
from jax import lax
from jax.experimental import pallas as pl
from jax.experimental.pallas import tpu as pltpu
from jax.sharding import PartitionSpec as P

MESH = pl.DeviceIdType.MESH
CW, CCW = 0, 1
PIECES = 4
HALVES = ((0, 1), (2, 3))


def place():
    r, p = lax.axis_index("req"), lax.axis_index("patch")
    return lax.div(r, 4), lax.rem(r, 4), lax.div(p, 8), lax.rem(lax.div(p, 2), 4), lax.rem(p, 2)


def at(x, z, y, c):
    z = lax.rem(z, 8)
    return (lax.rem(x, 4) * 4 + lax.rem(z, 4), lax.div(z, 4) * 8 + lax.rem(y, 4) * 2 + c)


def token_kernel(tok, w, down, up, bias, q_out, kv_out, held, relay, own_sem,
                 z1s, z1r, z2s, z2r, ys, yr, ss, sr):
    x, zl, zh, y, c = place()
    z = zh * 4 + zl
    rows = tok.shape[0]
    step = rows // PIECES
    other = 1 - c

    def shard(f, dy, cc):
        half = zh if f == 0 else 1 - zh
        return half * 8 + lax.rem(y + dy, 4) * 2 + cc

    sibling = at(x, z, y, other)
    ring = (at(x, z, y + 1, c), at(x, z, y + 3, c))
    zring = (at(x, z + 2, y, c), at(x, z + 6, y, c))

    barrier = pltpu.get_barrier_semaphore()
    for who in (sibling, *ring, *zring):
        pl.semaphore_signal(barrier, inc=1, device_id=who, device_id_type=MESH)
    pl.semaphore_wait(barrier, 5)

    def span(k):
        return pl.ds(k * step, step)

    def remote(src, dst, send, recv, who):
        return pltpu.make_async_remote_copy(
            src_ref=src, dst_ref=dst, send_sem=send, recv_sem=recv, device_id=who, device_id_type=MESH)

    started = []

    def go(copy):
        copy.start()
        started.append(copy)

    def source(f, k):
        return tok.at[span(k)] if f == 0 else held.at[shard(1, 0, c), span(k)]

    def y_copy(f, way, j):
        if j < 4:
            p, k, src = shard(f, 0, c), j, source(f, j)
        else:
            k = HALVES[way][j - 4]
            p = shard(f, 3 if way == CW else 1, c)
            src = held.at[p, span(k)]
        return remote(src, held.at[p, span(k)], ys.at[f, way, j], yr.at[f, way, j], ring[way])

    def y_arrived(f, way, j):
        if j < 4:
            p, k = shard(f, 3 if way == CW else 1, c), j
        else:
            p, k = shard(f, 2, c), HALVES[way][j - 4]
        piece = held.at[p, span(k)]
        remote(piece, piece, ys.at[f, way, j], yr.at[f, way, j], ring[way]).wait_recv()

    def s_copy(f, dy, k):
        src = tok.at[span(k)] if (f == 0 and dy == 0) else held.at[shard(f, dy, c), span(k)]
        return remote(src, held.at[shard(f, dy, c), span(k)], ss.at[f, dy, k], sr.at[f, dy, k], sibling)

    def s_arrived(f, dy, k):
        piece = held.at[shard(f, dy, other), span(k)]
        remote(piece, piece, ss.at[f, dy, k], sr.at[f, dy, k], sibling).wait_recv()

    def z1_copy(k):
        way = 0 if k < 2 else 1
        return remote(tok.at[span(k)], relay.at[k], z1s.at[k], z1r.at[k], zring[way])

    def z2_copy(k):
        way = 0 if k < 2 else 1
        oz = lax.rem(z + (6 if way == 0 else 2), 8)
        p = lax.div(oz, 4) * 8 + y * 2 + c
        return remote(relay.at[k], held.at[p, span(k)], z2s.at[k], z2r.at[k], zring[way])

    def z1_arrived(k):
        remote(relay.at[k], relay.at[k], z1s.at[k], z1r.at[k], sibling).wait_recv()

    def z2_arrived(k):
        piece = held.at[shard(1, 0, c), span(k)]
        remote(piece, piece, z2s.at[k], z2r.at[k], sibling).wait_recv()

    def project(ref, p):
        t = ref[...]
        low = lax.dot_general(t, down[...], (((1,), (1,)), ((), ())), preferred_element_type=jnp.float32)
        acc = jnp.dot(t, w[...], preferred_element_type=jnp.float32)
        acc = acc + jnp.dot(low.astype(jnp.bfloat16), up[...], preferred_element_type=jnp.float32)
        acc = acc + bias[...].astype(jnp.float32)
        here = pl.ds(pl.multiple_of(p * rows, rows), rows)
        q_out[here, :] = (acc[:, :128] * QSCALE).astype(jnp.bfloat16)
        kv_out[here, :] = acc[:, 128:].astype(jnp.bfloat16)

    def project_shard(f, dy, cc):
        p = shard(f, dy, cc)
        project(held.at[p], p)

    def take_y(f, way, j):
        y_arrived(f, way, j)
        if j < 4:
            if j in HALVES[way]:
                go(y_copy(f, way, 4 + HALVES[way].index(j)))
            go(s_copy(f, 3 if way == CW else 1, j))
        else:
            go(s_copy(f, 2, HALVES[way][j - 4]))

    def relay_on(k):
        z1_arrived(k)
        go(z2_copy(k))

    def take_z(k):
        z2_arrived(k)
        go(y_copy(1, CW, k))
        go(y_copy(1, CCW, k))
        go(s_copy(1, 0, k))

    def sib_ready(f, dy):
        for k in range(PIECES):
            s_arrived(f, dy, k)
        project_shard(f, dy, other)

    for k in (0, 2, 1, 3):
        go(z1_copy(k))
    for j in range(4):
        go(y_copy(0, CW, j))
        go(y_copy(0, CCW, (2, 3, 0, 1)[j]))
    for k in range(PIECES):
        go(s_copy(0, 0, k))

    project(tok, shard(0, 0, c))
    take_y(0, CW, 0)
    take_y(0, CCW, 2)
    sib_ready(0, 0)
    relay_on(0)
    relay_on(2)
    take_y(0, CW, 1)
    take_y(0, CCW, 3)
    take_y(0, CW, 2)
    take_y(0, CCW, 0)
    relay_on(1)
    relay_on(3)
    take_y(0, CW, 3)
    take_y(0, CCW, 1)
    project_shard(0, 3, c)
    project_shard(0, 1, c)
    take_z(0)
    take_z(2)
    sib_ready(0, 3)
    sib_ready(0, 1)
    take_y(0, CW, 4)
    take_y(0, CCW, 4)
    take_y(0, CW, 5)
    take_y(0, CCW, 5)
    take_y(1, CW, 0)
    take_y(1, CCW, 2)
    project_shard(0, 2, c)
    take_z(1)
    take_z(3)
    project_shard(1, 0, c)
    take_y(1, CW, 2)
    take_y(1, CCW, 0)
    sib_ready(0, 2)
    sib_ready(1, 0)
    take_y(1, CW, 1)
    take_y(1, CCW, 3)
    take_y(1, CW, 4)
    take_y(1, CCW, 4)
    take_y(1, CW, 3)
    take_y(1, CCW, 1)
    project_shard(1, 3, c)
    project_shard(1, 1, c)
    take_y(1, CW, 5)
    take_y(1, CCW, 5)
    sib_ready(1, 3)
    sib_ready(1, 1)
    project_shard(1, 2, c)
    sib_ready(1, 2)
    for copy in started:
        copy.wait_send()


QSCALE = math.log2(math.e) / math.sqrt(128)


def gather_project(tok, w, down, up, bias):
    rows, width = tok.shape
    dma = pltpu.SemaphoreType.DMA
    vmem = pl.BlockSpec(memory_space=pltpu.VMEM)
    return pl.pallas_call(
        token_kernel,
        out_shape=(jax.ShapeDtypeStruct((16 * rows, 128), jnp.bfloat16),
                   jax.ShapeDtypeStruct((16 * rows, 256), jnp.bfloat16)),
        in_specs=[vmem] * 5,
        out_specs=(vmem, vmem),
        scratch_shapes=[
            pltpu.VMEM((16, rows, width), jnp.bfloat16),
            pltpu.VMEM((PIECES, rows // PIECES, width), jnp.bfloat16),
            dma,
            dma((4,)), dma((4,)), dma((4,)), dma((4,)),
            dma((2, 2, 6)), dma((2, 2, 6)),
            dma((2, 4, 4)), dma((2, 4, 4)),
        ],
        compiler_params=pltpu.CompilerParams(
            collective_id=0, has_side_effects=True, vmem_limit_bytes=48 * 2**20),
        name="tokens_to_projection",
    )(tok, w, down, up, bias)


CHUNKS = 8


def pick(values, index):
    out = values[0]
    for n in range(1, len(values)):
        out = jnp.where(index == n, values[n], out)
    return out


def exchange_kernel(info, kv, out, xin, rs, rr, ls, lr, xout,
                    x1s, x1r, rsend, rrecv, lsend, lrecv, x2s, x2r):
    x, zl, zh, y, c = place()
    z = zh * 4 + zl
    length = kv.shape[0]
    part = length // (4 * CHUNKS)
    xs = [at(x + d, z, y, c) for d in range(4)]
    right, left = at(x, zh * 4 + lax.rem(zl + 1, 4), y, c), at(x, zh * 4 + lax.rem(zl + 3, 4), y, c)

    barrier = pltpu.get_barrier_semaphore()
    for who in (*xs[1:], right, left):
        pl.semaphore_signal(barrier, inc=1, device_id=who, device_id_type=MESH)
    pl.semaphore_wait(barrier, 5)

    def remote(src, dst, send, recv, who):
        return pltpu.make_async_remote_copy(
            src_ref=src, dst_ref=dst, send_sem=send, recv_sem=recv, device_id=who, device_id_type=MESH)

    def rows(ch, q):
        return pl.ds(pl.multiple_of((ch * 4 + q) * part, part), part)

    def x1_copy(ch, d):
        q = lax.rem(x + d, 4)
        return remote(kv.at[rows(ch, q)], xin.at[ch, x], x1s.at[ch, d], x1r.at[ch, 4 - d], xs[d])

    def x1_arrived(ch, d):
        piece = xin.at[ch, lax.rem(x + d, 4)]
        return remote(piece, piece, x1s.at[ch, d], x1r.at[ch, d], xs[d])

    def x2_copy(ch, d):
        return remote(xout.at[ch, d], out.at[rows(ch, x)], x2s.at[ch, d], x2r.at[ch, 4 - d], xs[d])

    def x2_arrived(ch, d):
        piece = out.at[rows(ch, lax.rem(x + d, 4))]
        return remote(piece, piece, x2s.at[ch, d], x2r.at[ch, d], xs[d])

    def r_copy(ch):
        return remote(rs.at[ch], rr.at[ch], rsend.at[ch], rrecv.at[ch], right)

    def l_copy(ch):
        return remote(ls.at[ch], lr.at[ch], lsend.at[ch], lrecv.at[ch], left)

    def begin(ch, carry):
        for d in (2, 1, 3):
            x1_copy(ch, d).start()
        xin[ch, x] = kv[rows(ch, x), :]
        return carry

    lax.fori_loop(0, CHUNKS, begin, 0)

    def mine(ch, slot):
        held = [xin[ch, n] for n in range(4)]
        return pick(held, info[0, slot])

    def flow(ch, incoming, sendbuf, copy, has_in, has_out):
        @pl.when(has_in)
        def _():
            remote(incoming.at[ch], incoming.at[ch], rsend.at[ch],
                   (rrecv if incoming is rr else lrecv).at[ch], right).wait_recv()

        @pl.when(has_out)
        def _():
            for slot in range(4):
                sendbuf[ch, slot] = jnp.where(info[1, slot] == 1, mine(ch, slot), incoming[ch, slot])
            copy(ch).start()

    def step(t, carry):
        @pl.when(t < CHUNKS)
        def _():
            for d in (1, 3, 2):
                x1_arrived(t, d).wait_recv()

        rc = t - zl
        @pl.when((rc >= 0) & (rc < CHUNKS))
        def _():
            flow(rc, rr, rs, r_copy, zl > 0, zl < 3)

        lc = t - (3 - zl)
        @pl.when((lc >= 0) & (lc < CHUNKS))
        def _():
            flow(lc, lr, ls, l_copy, zl < 3, zl > 0)

        ch = t - 3
        @pl.when(ch >= 0)
        def _():
            final = []
            for slot in range(4):
                far = jnp.where(info[1, slot] == 2, rr[ch, slot], lr[ch, slot])
                final.append(jnp.where(info[1, slot] == 1, mine(ch, slot), far))
            for d in (2, 1, 3):
                xout[ch, d] = pick(final, info[2, d])
                x2_copy(ch, d).start()
            out[rows(ch, x), :] = pick(final, info[2, 0])
        return carry

    lax.fori_loop(0, CHUNKS + 3, step, 0)

    def end(ch, carry):
        for d in (1, 3, 2):
            x2_arrived(ch, d).wait_recv()
            x1_copy(ch, d).wait_send()
            x2_copy(ch, d).wait_send()

        @pl.when(zl < 3)
        def _():
            r_copy(ch).wait_send()

        @pl.when(zl > 0)
        def _():
            l_copy(ch).wait_send()
        return carry

    lax.fori_loop(0, CHUNKS, end, 0)


def routes(references, pairing):
    r = lax.axis_index("req")
    x, zl = r // 4, r % 4
    plane = references % 4
    side = jnp.where(plane == zl, 1, jnp.where(plane < zl, 2, 0))
    slots = jnp.stack([pairing[((x + d) % 4) * 4 + zl] for d in range(4)])
    return jnp.stack([references // 4, side, slots]).astype(jnp.int32)


def exchange(info, kv):
    length, width = kv.shape
    part = length // (4 * CHUNKS)
    dma = pltpu.SemaphoreType.DMA
    vmem = pl.BlockSpec(memory_space=pltpu.VMEM)
    buf = pltpu.VMEM((CHUNKS, 4, part, width), kv.dtype)
    return pl.pallas_call(
        exchange_kernel,
        out_shape=jax.ShapeDtypeStruct((length, width), kv.dtype),
        in_specs=[pl.BlockSpec(memory_space=pltpu.SMEM), vmem],
        out_specs=vmem,
        scratch_shapes=[buf] * 6 + [dma((CHUNKS, 4)), dma((CHUNKS, 4))] + [dma((CHUNKS,))] * 4
        + [dma((CHUNKS, 4)), dma((CHUNKS, 4))],
        compiler_params=pltpu.CompilerParams(
            collective_id=1, has_side_effects=True, vmem_limit_bytes=48 * 2**20),
        name="reference_keys",
    )(info, kv)


TILE = 128
GROUP = 4


def attend_kernel(count, klist, vlist, q, own, theirs, out, keys, values, scores):
    tiles = q.shape[0] // TILE
    length = q.shape[0]

    def rows(t):
        return pl.ds(pl.multiple_of(t * TILE, TILE), TILE)

    def fill(t, carry):
        for ref, base in ((own, 0), (theirs, tiles)):
            keys[rows(base + t), :] = ref[rows(t), :TILE]
            values[rows(base + t), :TILE] = ref[rows(t), TILE:]
            values[rows(base + t), TILE:] = jnp.ones((TILE, TILE), jnp.bfloat16)
        return carry

    lax.fori_loop(0, tiles, fill, 0)
    values[rows(2 * tiles), :] = jnp.zeros((TILE, 2 * TILE), jnp.bfloat16)

    def tile(i, carry):
        qt = q[rows(i), :]
        groups = count[i]

        def first(g, top):
            for n in range(GROUP):
                kt = keys[rows(klist[i, g * GROUP + n]), :]
                s = lax.dot_general(qt, kt, (((1,), (1,)), ((), ())), preferred_element_type=jnp.float32)
                scores[g * GROUP + n] = s
                top = jnp.maximum(top, s)
            return top

        top = lax.fori_loop(0, groups, first, jnp.full((TILE, TILE), -jnp.inf, jnp.float32))
        top = jnp.max(top, axis=1, keepdims=True)

        def second(g, acc):
            for n in range(GROUP):
                p = jnp.exp2(scores[g * GROUP + n] - top).astype(jnp.bfloat16)
                acc = acc + jnp.dot(p, values[rows(vlist[i, g * GROUP + n]), :], preferred_element_type=jnp.float32)
            return acc

        acc = lax.fori_loop(0, groups, second, jnp.zeros((TILE, 2 * TILE), jnp.float32))
        out[rows(i), :] = (acc[:, :TILE] / acc[:, TILE:]).astype(jnp.bfloat16)
        return carry

    lax.fori_loop(0, tiles, tile, 0)


def lists(mask):
    tiles = mask.shape[0]
    i = lax.broadcasted_iota(jnp.int32, (tiles, 2 * tiles), 0)
    j = lax.broadcasted_iota(jnp.int32, (tiles, 2 * tiles), 1)
    allow = ((mask == 1) | (i == j)).astype(jnp.int32)
    total = jnp.sum(allow, axis=1)
    before = jnp.sum(jnp.where(j[0][:, None] < j[0][None, :], allow[:, :, None], 0), axis=1)
    at = (before[:, :, None] == j[0][None, None, :]) & (allow[:, :, None] == 1)
    order = jnp.sum(jnp.where(at, j[:, :, None], 0), axis=1)
    used = j < total[:, None]
    klist = jnp.where(used, order, i)
    vlist = jnp.where(used, order, 2 * tiles)
    return (total + GROUP - 1) // GROUP, klist, vlist


def attend(mask, q, own, theirs):
    length = q.shape[0]
    tiles = length // TILE
    vmem = pl.BlockSpec(memory_space=pltpu.VMEM)
    smem = pl.BlockSpec(memory_space=pltpu.SMEM)
    count, klist, vlist = lists(mask)
    return pl.pallas_call(
        attend_kernel,
        out_shape=jax.ShapeDtypeStruct((length, TILE), jnp.bfloat16),
        in_specs=[smem] * 3 + [vmem] * 3,
        out_specs=vmem,
        scratch_shapes=[
            pltpu.VMEM((2 * length, TILE), jnp.bfloat16),
            pltpu.VMEM((2 * length + TILE, 2 * TILE), jnp.bfloat16),
            pltpu.VMEM((2 * tiles, TILE, TILE), jnp.float32),
        ],
        compiler_params=pltpu.CompilerParams(vmem_limit_bytes=48 * 2**20),
        name="attention",
    )(count, klist, vlist, q, own, theirs)


def on_device(tokens, projection_weight, projection_bias, adapter_down_weight, adapter_up_weight,
              tile_allow_mask, references, pairing):
    q, own = gather_project(tokens[0], projection_weight[:, 0], adapter_down_weight[0].T,
                            adapter_up_weight[0, :, 0], projection_bias)
    theirs = exchange(routes(references, pairing), own)
    mixed = attend(tile_allow_mask[0], q, own, theirs)
    return lax.all_to_all(mixed, "patch", split_axis=0, concat_axis=1, tiled=True)[None]


def solution(mesh):
    in_specs = (
        P("req", "patch", None),
        P(None, "patch", None),
        P("patch", None),
        P("req", None, None),
        P("req", None, "patch", None),
        P("req", None, None),
        P(),
        P(),
    )
    return jax.shard_map(
        on_device, mesh=mesh, in_specs=in_specs, out_specs=P("req", "patch", None), check_vma=False
    )
```

```python
import math

import jax
import jax.numpy as jnp
from jax import lax
from jax.experimental import pallas as pl
from jax.experimental.pallas import tpu as pltpu
from jax.sharding import PartitionSpec as P

MESH = pl.DeviceIdType.MESH
CW, CCW = 0, 1
PIECES = 4
HALVES = ((0, 1), (2, 3))
TILE = 128
HEAD = 128
CHUNKS = 8
QROWS = 512
KROWS = 1024
KSTEP = 256
LOW = -1e30
QSCALE = math.log2(math.e) / math.sqrt(HEAD)
ORDER = ((0, 0), (0, 1), (3, 0), (1, 0), (3, 1), (1, 1), (2, 0), (2, 1))
MIRROR = (0, 1, 3, 2, 5, 4, 6, 7)


def place():
    r, p = lax.axis_index("req"), lax.axis_index("patch")
    return lax.div(r, 4), lax.rem(r, 4), lax.div(p, 8), lax.rem(lax.div(p, 2), 4), lax.rem(p, 2)


def at(x, z, y, c):
    z = lax.rem(z, 8)
    return (lax.rem(x, 4) * 4 + lax.rem(z, 4), lax.div(z, 4) * 8 + lax.rem(y, 4) * 2 + c)


def pick(values, index):
    out = values[0]
    for n in range(1, len(values)):
        out = jnp.where(index == n, values[n], out)
    return out


def block_kernel(references, pairing, mask, bias, tok_hbm, w_hbm, down_hbm, up_hbm, out,
                 held, relay, w, down, up, q, kt, va, kv, refkv, xin, rs, rr, ls, lr, xout,
                 s, top_all, acc_all, mixed,
                 lsem, z1s, z1r, z2s, z2r, ys, yr, ss, sr,
                 x1s, x1r, rsend, rrecv, lsend, lrecv, x2s, x2r, os, orv):
    x, zl, zh, y, c = place()
    z = zh * 4 + zl
    rows = tok_hbm.shape[0]
    step = rows // PIECES
    part = 2 * rows // 4
    other = 1 - c
    me = zh * 8 + y * 2 + c

    def shard(f, dy, cc):
        half = zh if f == 0 else 1 - zh
        return half * 8 + lax.rem(y + dy, 4) * 2 + cc

    def logical(j):
        f, (dy, o) = j // 8, ORDER[j % 8]
        return f, dy, (other if o else c)

    tok = held.at[me]
    local = [
        pltpu.make_async_copy(tok_hbm, tok, lsem.at[0]),
        pltpu.make_async_copy(w_hbm, w, lsem.at[1]),
        pltpu.make_async_copy(down_hbm, down, lsem.at[2]),
        pltpu.make_async_copy(up_hbm, up, lsem.at[3]),
    ]
    for copy in local:
        copy.start()

    sibling = at(x, z, y, other)
    ring = (at(x, z, y + 1, c), at(x, z, y + 3, c))
    zring = (at(x, z + 2, y, c), at(x, z + 6, y, c))
    xs = [at(x + d, z, y, c) for d in range(4)]
    right = at(x, zh * 4 + lax.rem(zl + 1, 4), y, c)
    left = at(x, zh * 4 + lax.rem(zl + 3, 4), y, c)
    owners = []
    for j in range(16):
        f, dy, cc = logical(j)
        owners.append((x * 4 + zl, shard(f, dy, cc)))

    barrier = pltpu.get_barrier_semaphore()
    everyone = (*owners[1:], *zring, *xs[1:], right, left)
    for who in everyone:
        pl.semaphore_signal(barrier, inc=1, device_id=who, device_id_type=MESH)
    pl.semaphore_wait(barrier, len(everyone))

    def remote(src, dst, send, recv, who):
        return pltpu.make_async_remote_copy(
            src_ref=src, dst_ref=dst, send_sem=send, recv_sem=recv, device_id=who, device_id_type=MESH)

    started = []

    def go(copy):
        copy.start()
        started.append(copy)

    def span(k):
        return pl.ds(k * step, step)

    def y_copy(f, way, j):
        if j < 4:
            p, k = shard(f, 0, c), j
        else:
            p, k = shard(f, 3 if way == CW else 1, c), HALVES[way][j - 4]
        piece = held.at[p, span(k)]
        return remote(piece, piece, ys.at[f, way, j], yr.at[f, way, j], ring[way])

    def y_arrived(f, way, j):
        if j < 4:
            p, k = shard(f, 3 if way == CW else 1, c), j
        else:
            p, k = shard(f, 2, c), HALVES[way][j - 4]
        piece = held.at[p, span(k)]
        remote(piece, piece, ys.at[f, way, j], yr.at[f, way, j], ring[way]).wait_recv()

    def s_copy(f, dy, k):
        piece = held.at[shard(f, dy, c), span(k)]
        return remote(piece, piece, ss.at[f, dy, k], sr.at[f, dy, k], sibling)

    def s_arrived(f, dy, k):
        piece = held.at[shard(f, dy, other), span(k)]
        remote(piece, piece, ss.at[f, dy, k], sr.at[f, dy, k], sibling).wait_recv()

    def z1_copy(k):
        return remote(tok.at[span(k)], relay.at[k], z1s.at[k], z1r.at[k], zring[0 if k < 2 else 1])

    def z2_copy(k):
        way = 0 if k < 2 else 1
        oz = lax.rem(z + (6 if way == 0 else 2), 8)
        p = lax.div(oz, 4) * 8 + y * 2 + c
        return remote(relay.at[k], held.at[p, span(k)], z2s.at[k], z2r.at[k], zring[way])

    def take_y(f, way, j):
        y_arrived(f, way, j)
        if j < 4:
            if j in HALVES[way]:
                go(y_copy(f, way, 4 + HALVES[way].index(j)))
            go(s_copy(f, 3 if way == CW else 1, j))
        else:
            go(s_copy(f, 2, HALVES[way][j - 4]))

    def relay_on(k):
        remote(relay.at[k], relay.at[k], z1s.at[k], z1r.at[k], sibling).wait_recv()
        go(z2_copy(k))

    def take_z(k):
        piece = held.at[shard(1, 0, c), span(k)]
        remote(piece, piece, z2s.at[k], z2r.at[k], sibling).wait_recv()
        go(y_copy(1, CW, k))
        go(y_copy(1, CCW, k))
        go(s_copy(1, 0, k))

    def project(j):
        f, dy, cc = logical(j)
        if ORDER[j % 8][1]:
            for k in range(PIECES):
                s_arrived(f, dy, k)
        t = held[shard(f, dy, cc)]
        low = lax.dot_general(t, down[...], (((1,), (1,)), ((), ())), preferred_element_type=jnp.float32)
        acc = jnp.dot(t, w[...], preferred_element_type=jnp.float32)
        acc = acc + jnp.dot(low.astype(jnp.bfloat16), up[...], preferred_element_type=jnp.float32)
        acc = acc + bias[...].astype(jnp.float32)
        here = slice(j * rows, (j + 1) * rows)
        q[here, :HEAD] = (acc[:, :HEAD] * QSCALE).astype(jnp.bfloat16)
        column = lax.broadcasted_iota(jnp.int32, (rows, HEAD), 1)
        q[here, HEAD:] = jnp.where(column == j, 1.0, 0.0).astype(jnp.bfloat16)
        kv[here, :] = acc[:, HEAD:].astype(jnp.bfloat16)
        kt[:HEAD, here] = acc[:, HEAD:2 * HEAD].T.astype(jnp.bfloat16)
        va[here, :HEAD] = acc[:, 2 * HEAD:].astype(jnp.bfloat16)

    def piece_rows(ch, n):
        return pl.ds(pl.multiple_of(ch * (4 * part) + n * part, part), part)

    def x1_copy(ch, d):
        return remote(kv.at[piece_rows(ch, lax.rem(x + d, 4))], xin.at[ch, x], x1s.at[ch, d], x1r.at[ch, 4 - d], xs[d])

    def x2_copy(ch, d):
        return remote(xout.at[ch, d], refkv.at[piece_rows(ch, x)], x2s.at[ch, d], x2r.at[ch, 4 - d], xs[d])

    def r_copy(ch):
        return remote(rs.at[ch], rr.at[ch], rsend.at[ch], rrecv.at[ch], right)

    def l_copy(ch):
        return remote(ls.at[ch], lr.at[ch], lsend.at[ch], lrecv.at[ch], left)

    columns = [lax.div(references[n], 4) for n in range(4)]
    planes = [lax.rem(references[n], 4) for n in range(4)]
    slots = [pairing[lax.rem(x + d, 4) * 4 + zl] for d in range(4)]

    def keys_send(ch):
        for d in (2, 1, 3):
            go(x1_copy(ch, d))
        xin[ch, x] = kv[piece_rows(ch, x), :]

    def mine(ch, slot):
        return pick([xin[ch, n] for n in range(4)], columns[slot])

    def keys_step(t):
        if t < CHUNKS:
            for d in (1, 3, 2):
                piece = xin.at[t, lax.rem(x + d, 4)]
                remote(piece, piece, x1s.at[t, d], x1r.at[t, d], xs[d]).wait_recv()

        rc = t - zl

        @pl.when((rc >= 0) & (rc < CHUNKS))
        def _():
            @pl.when(zl > 0)
            def _():
                remote(rr.at[rc], rr.at[rc], rsend.at[rc], rrecv.at[rc], left).wait_recv()

            @pl.when(zl < 3)
            def _():
                for slot in range(4):
                    rs[rc, slot] = jnp.where(planes[slot] == zl, mine(rc, slot), rr[rc, slot])
                r_copy(rc).start()

        lc = t - (3 - zl)

        @pl.when((lc >= 0) & (lc < CHUNKS))
        def _():
            @pl.when(zl < 3)
            def _():
                remote(lr.at[lc], lr.at[lc], lsend.at[lc], lrecv.at[lc], right).wait_recv()

            @pl.when(zl > 0)
            def _():
                for slot in range(4):
                    ls[lc, slot] = jnp.where(planes[slot] == zl, mine(lc, slot), lr[lc, slot])
                l_copy(lc).start()

        ch = t - 3
        if ch >= 0:
            final = []
            for slot in range(4):
                far = jnp.where(planes[slot] < zl, rr[ch, slot], lr[ch, slot])
                final.append(jnp.where(planes[slot] == zl, mine(ch, slot), far))
            for d in (2, 1, 3):
                xout[ch, d] = pick(final, slots[d])
                go(x2_copy(ch, d))
            refkv[piece_rows(ch, x), :] = pick(final, slots[0])

    def keys_take(ch):
        for d in (1, 3, 2):
            piece = refkv.at[piece_rows(ch, lax.rem(x + d, 4))]
            remote(piece, piece, x2s.at[ch, d], x2r.at[ch, d], xs[d]).wait_recv()
        size = 4 * part
        got = refkv[ch * size:(ch + 1) * size, :]
        base = 16 * rows + ch * size
        kt[:HEAD, base:base + size] = got[:, :HEAD].astype(jnp.float32).T.astype(jnp.bfloat16)
        va[base:base + size, :HEAD] = got[:, HEAD:]

    def unit(b, block, first=False):
        here = pl.ds(pl.multiple_of(b * QROWS, QROWS), QROWS)
        qt = q[here, :]
        top = None
        for n in range(KROWS // KSTEP):
            k0 = block * KROWS + n * KSTEP
            score = jnp.dot(qt, kt[:, k0:k0 + KSTEP], preferred_element_type=jnp.float32)
            s[:, n * KSTEP:(n + 1) * KSTEP] = score
            for m in range(KSTEP // 128):
                piece = score[:, m * 128:(m + 1) * 128]
                top = piece if top is None else jnp.maximum(top, piece)
        top = jnp.max(top, axis=1, keepdims=True)
        acc = None
        if not first:
            old = top_all[here, :1]
            top = jnp.maximum(top, old)
            acc = acc_all[here, :] * jnp.exp2(old - top)
        top_all[here, :] = jnp.broadcast_to(top, (QROWS, 128))
        for n in range(KROWS // KSTEP):
            k0 = block * KROWS + n * KSTEP
            weight = jnp.exp2((s[:, n * KSTEP:(n + 1) * KSTEP] - top).astype(jnp.bfloat16))
            more = jnp.dot(weight, va[k0:k0 + KSTEP, :], preferred_element_type=jnp.float32)
            acc = more if acc is None else acc + more
        return here, acc

    def units(b0, b1, block, first=False):
        def body(b, carry):
            here, acc = unit(b, block, first)
            acc_all[here, :] = acc
            return carry

        lax.fori_loop(b0, b1, body, 0)

    def my_columns():
        return pl.ds(pl.multiple_of(me * HEAD, HEAD), HEAD)

    def o_copy(j):
        place_there = (j // 8) * 8 + MIRROR[j % 8]
        return remote(mixed.at[j], out.at[:, my_columns()], os.at[j], orv.at[place_there], owners[j])

    def finish(b):
        here, acc = unit(b, 3)
        result = (acc[:, :HEAD] / acc[:, HEAD:HEAD + 1]).astype(jnp.bfloat16)
        for n in range(QROWS // TILE):
            j = b * (QROWS // TILE) + n
            if j == 0:
                out[:, my_columns()] = result[:TILE]
            else:
                mixed[j] = result[n * TILE:(n + 1) * TILE]
                go(o_copy(j))

    local[0].wait()
    for k in (0, 2, 1, 3):
        go(z1_copy(k))
    for j in range(4):
        go(y_copy(0, CW, j))
        go(y_copy(0, CCW, (2, 3, 0, 1)[j]))
    for k in range(PIECES):
        go(s_copy(0, 0, k))

    tiles = mask.shape[0]
    tile_row = lax.broadcasted_iota(jnp.int32, (tiles, 2 * tiles), 0)
    tile_col = lax.broadcasted_iota(jnp.int32, (tiles, 2 * tiles), 1)
    allow = jnp.where((mask[...] == 1) | (tile_row == tile_col), 1.0, 0.0).astype(jnp.bfloat16)

    def order_of(tile):
        far = jnp.where(lax.div(tile, 8) == zh, 0, 8)
        dy = lax.rem(lax.rem(lax.div(tile, 2), 4) + 4 - y, 4)
        o = jnp.where(lax.rem(tile, 2) == c, 0, 1)
        near = jnp.where(dy == 0, o, jnp.where(dy == 2, 6 + o, jnp.where(dy == 3, 2, 3) + 2 * o))
        return far + near

    turn = jnp.where(
        order_of(lax.broadcasted_iota(jnp.int32, (tiles, tiles), 1)) == lax.broadcasted_iota(jnp.int32, (tiles, tiles), 0),
        1.0, 0.0).astype(jnp.bfloat16)
    turned = jnp.dot(turn, allow, preferred_element_type=jnp.float32).astype(jnp.bfloat16)
    spread_shape = (tiles, tiles * TILE)
    spread = jnp.where(
        order_of(lax.broadcasted_iota(jnp.int32, spread_shape, 0)) == lax.div(lax.broadcasted_iota(jnp.int32, spread_shape, 1), TILE),
        1.0, 0.0).astype(jnp.bfloat16)
    for side in range(2):
        wide = jnp.dot(turned[:, side * tiles:(side + 1) * tiles], spread, preferred_element_type=jnp.float32)
        kt[HEAD:HEAD + tiles, side * tiles * TILE:(side + 1) * tiles * TILE] = jnp.where(wide > 0.5, 0.0, LOW).astype(jnp.bfloat16)
    kt[HEAD + tiles:, :] = jnp.zeros((HEAD - tiles, 2 * tiles * TILE), jnp.bfloat16)
    va[:, HEAD:] = jnp.ones((2 * tiles * TILE, HEAD), jnp.bfloat16)

    for copy in local[1:]:
        copy.wait()
    project(0)
    take_y(0, CW, 0)
    take_y(0, CCW, 2)
    project(1)
    keys_send(0)
    relay_on(0)
    relay_on(2)
    take_y(0, CW, 1)
    take_y(0, CCW, 3)
    take_y(0, CW, 2)
    take_y(0, CCW, 0)
    relay_on(1)
    relay_on(3)
    take_y(0, CW, 3)
    take_y(0, CCW, 1)
    project(2)
    project(3)
    keys_send(1)
    take_z(0)
    take_z(2)
    keys_step(0)
    project(4)
    project(5)
    keys_send(2)
    take_y(0, CW, 4)
    take_y(0, CCW, 4)
    take_y(0, CW, 5)
    take_y(0, CCW, 5)
    take_y(1, CW, 0)
    take_y(1, CCW, 2)
    keys_step(1)
    project(6)
    take_z(1)
    take_z(3)
    project(8)
    take_y(1, CW, 2)
    take_y(1, CCW, 0)
    project(7)
    keys_send(3)
    keys_step(2)
    project(9)
    keys_send(4)
    take_y(1, CW, 1)
    take_y(1, CCW, 3)
    keys_step(3)
    take_y(1, CW, 4)
    take_y(1, CCW, 4)
    units(0, 2, 0, True)
    take_y(1, CW, 3)
    take_y(1, CCW, 1)
    keys_step(4)
    project(10)
    project(11)
    keys_send(5)
    take_y(1, CW, 5)
    take_y(1, CCW, 5)
    keys_step(5)
    project(12)
    project(13)
    keys_send(6)
    project(14)
    project(15)
    keys_send(7)
    keys_step(6)
    units(2, 4, 0, True)
    keys_step(7)
    for ch in range(4):
        keys_take(ch)
    units(0, 2, 1)
    keys_step(8)
    units(2, 4, 1)
    keys_step(9)
    units(0, 2, 2)
    keys_step(10)
    units(2, 4, 2)
    for ch in range(4, 8):
        keys_take(ch)
    for b in (2, 3, 0, 1):
        finish(b)
    for j in range(1, 16):
        f, dy, cc = logical(j)
        there = out.at[:, pl.ds(pl.multiple_of(shard(f, dy, cc) * HEAD, HEAD), HEAD)]
        remote(there, there, os.at[j], orv.at[j], owners[j]).wait_recv()
    for copy in started:
        copy.wait_send()

    @pl.when(zl < 3)
    def _():
        for ch in range(CHUNKS):
            r_copy(ch).wait_send()

    @pl.when(zl > 0)
    def _():
        for ch in range(CHUNKS):
            l_copy(ch).wait_send()


def whole_block(references, pairing, mask, bias, tok, w, down, up):
    rows, width = tok.shape
    length = 16 * rows
    dma = pltpu.SemaphoreType.DMA
    vmem = pl.BlockSpec(memory_space=pltpu.VMEM)
    smem = pl.BlockSpec(memory_space=pltpu.SMEM)
    anywhere = pl.BlockSpec(memory_space=pl.ANY)
    half = jnp.bfloat16
    pieces = pltpu.VMEM((CHUNKS, 4, rows // 2, 2 * HEAD), half)
    return pl.pallas_call(
        block_kernel,
        out_shape=jax.ShapeDtypeStruct((rows, 16 * HEAD), half),
        in_specs=[smem, smem, vmem, vmem] + [anywhere] * 4,
        out_specs=vmem,
        scratch_shapes=[
            pltpu.VMEM((16, rows, width), half),
            pltpu.VMEM((PIECES, rows // PIECES, width), half),
            pltpu.VMEM(w.shape, half),
            pltpu.VMEM(down.shape, half),
            pltpu.VMEM(up.shape, half),
            pltpu.VMEM((length, 2 * HEAD), half),
            pltpu.VMEM((2 * HEAD, 2 * length), half),
            pltpu.VMEM((2 * length, 2 * HEAD), half),
            pltpu.VMEM((length, 2 * HEAD), half),
            pltpu.VMEM((length, 2 * HEAD), half),
            pieces, pieces, pieces, pieces, pieces, pieces,
            pltpu.VMEM((QROWS, KROWS), jnp.float32),
            pltpu.VMEM((length, 128), jnp.float32),
            pltpu.VMEM((length, 2 * HEAD), jnp.float32),
            pltpu.VMEM((16, rows, HEAD), half),
            dma((4,)),
            dma((4,)), dma((4,)), dma((4,)), dma((4,)),
            dma((2, 2, 6)), dma((2, 2, 6)),
            dma((2, 4, 4)), dma((2, 4, 4)),
            dma((CHUNKS, 4)), dma((CHUNKS, 4)),
            dma((CHUNKS,)), dma((CHUNKS,)), dma((CHUNKS,)), dma((CHUNKS,)),
            dma((CHUNKS, 4)), dma((CHUNKS, 4)),
            dma((16,)), dma((16,)),
        ],
        compiler_params=pltpu.CompilerParams(
            collective_id=0, has_side_effects=True, vmem_limit_bytes=56 * 2**20),
        name="attention_block",
    )(references, pairing, mask, bias, tok, w, down, up)


def on_device(tokens, projection_weight, projection_bias, adapter_down_weight, adapter_up_weight,
              tile_allow_mask, references, pairing):
    return whole_block(references, pairing, tile_allow_mask[0], projection_bias, tokens[0],
                       projection_weight[:, 0], adapter_down_weight[0].T, adapter_up_weight[0, :, 0])[None]


def solution(mesh):
    in_specs = (
        P("req", "patch", None),
        P(None, "patch", None),
        P("patch", None),
        P("req", None, None),
        P("req", None, "patch", None),
        P("req", None, None),
        P(),
        P(),
    )
    return jax.shard_map(
        on_device, mesh=mesh, in_specs=in_specs, out_specs=P("req", "patch", None), check_vma=False
    )
```

```python
import math

import jax
import jax.numpy as jnp
from jax import lax
from jax.experimental import pallas as pl
from jax.experimental.pallas import tpu as pltpu
from jax.sharding import PartitionSpec as P

MESH = pl.DeviceIdType.MESH
CW, CCW = 0, 1
PIECES = 4
HALVES = ((0, 1), (2, 3))
TILE = 128
HEAD = 128
SIZES = (2, 2, 2, 2, 2, 2, 2, 1, 1)
STARTS = tuple(sum(SIZES[:n]) for n in range(len(SIZES)))
CHUNKS = len(SIZES)
LAG = 2
QROWS = 512
KROWS = 1024
KSTEP = 256
LOW = -1e30
OWN0, OWN1, REF0, REF1, LAST = (0, 1024), (1024, 2048), (2048, 3072), (3072, 3840), (3840, 4096)
QSCALE = math.log2(math.e) / math.sqrt(HEAD)
ORDER = ((0, 0), (0, 1), (3, 0), (1, 0), (3, 1), (1, 1), (2, 0), (2, 1))
MIRROR = (0, 1, 3, 2, 5, 4, 6, 7)


def place():
    r, p = lax.axis_index("req"), lax.axis_index("patch")
    return lax.div(r, 4), lax.rem(r, 4), lax.div(p, 8), lax.rem(lax.div(p, 2), 4), lax.rem(p, 2)


def at(x, z, y, c):
    z = lax.rem(z, 8)
    return (lax.rem(x, 4) * 4 + lax.rem(z, 4), lax.div(z, 4) * 8 + lax.rem(y, 4) * 2 + c)


def pick(values, index):
    out = values[0]
    for n in range(1, len(values)):
        out = jnp.where(index == n, values[n], out)
    return out


def block_kernel(references, pairing, mask, bias, tok_hbm, w_hbm, down_hbm, up_hbm, out,
                 held, relay, w, down, up, q, kt, va, kv, refkv, xin, chosen, rs, rr, ls, lr, xout,
                 s, top_all, acc_all, mixed,
                 lsem, z1s, z1r, z2s, z2r, ys, yr, ss, sr,
                 x1s, x1r, rsend, rrecv, lsend, lrecv, x2s, x2r, os, orv):
    x, zl, zh, y, c = place()
    z = zh * 4 + zl
    rows = tok_hbm.shape[0]
    step = rows // PIECES
    quarter = rows // 4
    other = 1 - c
    me = zh * 8 + y * 2 + c

    def shard(f, dy, cc):
        half = zh if f == 0 else 1 - zh
        return half * 8 + lax.rem(y + dy, 4) * 2 + cc

    def logical(j):
        f, (dy, o) = j // 8, ORDER[j % 8]
        return f, dy, (other if o else c)

    tok = held.at[me]
    local = [
        pltpu.make_async_copy(tok_hbm, tok, lsem.at[0]),
        pltpu.make_async_copy(w_hbm, w, lsem.at[1]),
        pltpu.make_async_copy(down_hbm, down, lsem.at[2]),
        pltpu.make_async_copy(up_hbm, up, lsem.at[3]),
    ]
    for copy in local:
        copy.start()

    sibling = at(x, z, y, other)
    ring = (at(x, z, y + 1, c), at(x, z, y + 3, c))
    zring = (at(x, z + 2, y, c), at(x, z + 6, y, c))
    xs = [at(x + d, z, y, c) for d in range(4)]
    right = at(x, zh * 4 + lax.rem(zl + 1, 4), y, c)
    left = at(x, zh * 4 + lax.rem(zl + 3, 4), y, c)
    owners = []
    for j in range(16):
        f, dy, cc = logical(j)
        owners.append((x * 4 + zl, shard(f, dy, cc)))

    barrier = pltpu.get_barrier_semaphore()
    everyone = (sibling, *ring, *zring, *xs[1:], right, left)
    for who in everyone:
        pl.semaphore_signal(barrier, inc=1, device_id=who, device_id_type=MESH)
    pl.semaphore_wait(barrier, len(everyone))

    def remote(src, dst, send, recv, who):
        return pltpu.make_async_remote_copy(
            src_ref=src, dst_ref=dst, send_sem=send, recv_sem=recv, device_id=who, device_id_type=MESH)

    started = []

    def go(copy):
        copy.start()
        started.append(copy)

    def span(k):
        return pl.ds(k * step, step)

    def y_copy(f, way, j):
        if j < 4:
            p, k = shard(f, 0, c), j
        else:
            p, k = shard(f, 3 if way == CW else 1, c), HALVES[way][j - 4]
        piece = held.at[p, span(k)]
        return remote(piece, piece, ys.at[f, way, j], yr.at[f, way, j], ring[way])

    def y_arrived(f, way, j):
        if j < 4:
            p, k = shard(f, 3 if way == CW else 1, c), j
        else:
            p, k = shard(f, 2, c), HALVES[way][j - 4]
        piece = held.at[p, span(k)]
        remote(piece, piece, ys.at[f, way, j], yr.at[f, way, j], ring[way]).wait_recv()

    def s_copy(f, dy, k):
        piece = held.at[shard(f, dy, c), span(k)]
        return remote(piece, piece, ss.at[f, dy, k], sr.at[f, dy, k], sibling)

    def s_arrived(f, dy, k):
        piece = held.at[shard(f, dy, other), span(k)]
        remote(piece, piece, ss.at[f, dy, k], sr.at[f, dy, k], sibling).wait_recv()

    def z1_copy(k):
        return remote(tok.at[span(k)], relay.at[k], z1s.at[k], z1r.at[k], zring[0 if k < 2 else 1])

    def z2_copy(k):
        way = 0 if k < 2 else 1
        oz = lax.rem(z + (6 if way == 0 else 2), 8)
        p = lax.div(oz, 4) * 8 + y * 2 + c
        return remote(relay.at[k], held.at[p, span(k)], z2s.at[k], z2r.at[k], zring[way])

    def take_y(f, way, j):
        y_arrived(f, way, j)
        if j < 4:
            if j in HALVES[way]:
                go(y_copy(f, way, 4 + HALVES[way].index(j)))
            go(s_copy(f, 3 if way == CW else 1, j))
        else:
            go(s_copy(f, 2, HALVES[way][j - 4]))

    def relay_on(k):
        remote(relay.at[k], relay.at[k], z1s.at[k], z1r.at[k], sibling).wait_recv()
        go(z2_copy(k))

    def take_z(k):
        piece = held.at[shard(1, 0, c), span(k)]
        remote(piece, piece, z2s.at[k], z2r.at[k], sibling).wait_recv()
        go(y_copy(1, CW, k))
        go(y_copy(1, CCW, k))
        go(s_copy(1, 0, k))

    def project(j):
        f, dy, cc = logical(j)
        if ORDER[j % 8][1]:
            for k in range(PIECES):
                s_arrived(f, dy, k)
        t = held[shard(f, dy, cc)]
        low = lax.dot_general(t, down[...], (((1,), (1,)), ((), ())), preferred_element_type=jnp.float32)
        acc = jnp.dot(t, w[...], preferred_element_type=jnp.float32)
        acc = acc + jnp.dot(low.astype(jnp.bfloat16), up[...], preferred_element_type=jnp.float32)
        acc = acc + bias[...].astype(jnp.float32)
        here = slice(j * rows, (j + 1) * rows)
        q[here, :HEAD] = (acc[:, :HEAD] * QSCALE).astype(jnp.bfloat16)
        column = lax.broadcasted_iota(jnp.int32, (rows, HEAD), 1)
        q[here, HEAD:] = jnp.where(column == j, 1.0, 0.0).astype(jnp.bfloat16)
        kv[here, :] = acc[:, HEAD:].astype(jnp.bfloat16)
        kt[:HEAD, here] = acc[:, HEAD:2 * HEAD].T.astype(jnp.bfloat16)
        va[here, :HEAD] = acc[:, 2 * HEAD:].astype(jnp.bfloat16)

    def size(ch):
        return SIZES[ch] * quarter

    def piece_rows(ch, n):
        return pl.ds(pl.multiple_of(STARTS[ch] * rows + n * size(ch), quarter), size(ch))

    def first(ch):
        return pl.ds(0, size(ch))

    def x1_copy(ch, d):
        return remote(kv.at[piece_rows(ch, lax.rem(x + d, 4))], xin.at[ch, x, first(ch)],
                      x1s.at[ch, d], x1r.at[ch, 4 - d], xs[d])

    def x2_copy(ch, d):
        return remote(xout.at[ch, d, first(ch)], refkv.at[piece_rows(ch, x)],
                      x2s.at[ch, d], x2r.at[ch, 4 - d], xs[d])

    def r_copy(ch):
        return remote(rs.at[ch, :, first(ch)], rr.at[ch, :, first(ch)], rsend.at[ch], rrecv.at[ch], right)

    def l_copy(ch):
        return remote(ls.at[ch, :, first(ch)], lr.at[ch, :, first(ch)], lsend.at[ch], lrecv.at[ch], left)

    columns = [lax.div(references[n], 4) for n in range(4)]
    planes = [lax.rem(references[n], 4) for n in range(4)]
    slots = [pairing[lax.rem(x + d, 4) * 4 + zl] for d in range(4)]

    def keys_send(ch):
        for d in (2, 1, 3):
            go(x1_copy(ch, d))
        xin[ch, x, first(ch)] = kv[piece_rows(ch, x), :]

    def is_mine(slot):
        return planes[slot] == zl

    def flow(ch, copy, incoming, outgoing, source, sink):
        if source:
            piece = incoming.at[ch, :, first(ch)]
            if incoming is rr:
                remote(piece, piece, rsend.at[ch], rrecv.at[ch], left).wait_recv()
            else:
                remote(piece, piece, lsend.at[ch], lrecv.at[ch], right).wait_recv()
        if sink:
            for slot in range(4):
                value = chosen[ch, slot, first(ch)]
                if source:
                    value = jnp.where(is_mine(slot), value, incoming[ch, slot, first(ch)])
                outgoing[ch, slot, first(ch)] = value
            copy(ch).start()

    def keys_step(t):
        if t < CHUNKS:
            for d in (1, 3, 2):
                piece = xin.at[t, lax.rem(x + d, 4), first(t)]
                remote(piece, piece, x1s.at[t, d], x1r.at[t, d], xs[d]).wait_recv()
            here = [xin[t, n, first(t)] for n in range(4)]
            for slot in range(4):
                chosen[t, slot, first(t)] = pick(here, columns[slot])

        for line in range(4):
            rc, lc = t - LAG * line, t - LAG * (3 - line)

            @pl.when(zl == line)
            def _():
                def rightward():
                    if 0 <= rc < CHUNKS:
                        flow(rc, r_copy, rr, rs, line > 0, line < 3)

                def leftward():
                    if 0 <= lc < CHUNKS:
                        flow(lc, l_copy, lr, ls, line < 3, line > 0)

                if line < 2:
                    rightward()
                    leftward()
                else:
                    leftward()
                    rightward()

        ch = t - 3 * LAG
        if 0 <= ch < CHUNKS:
            final = []
            for slot in range(4):
                far = jnp.where(planes[slot] < zl, rr[ch, slot, first(ch)], lr[ch, slot, first(ch)])
                final.append(jnp.where(is_mine(slot), chosen[ch, slot, first(ch)], far))
            for d in (2, 1, 3):
                xout[ch, d, first(ch)] = pick(final, slots[d])
                go(x2_copy(ch, d))
            refkv[piece_rows(ch, x), :] = pick(final, slots[0])

    def keys_take(ch):
        for d in (1, 3, 2):
            piece = refkv.at[piece_rows(ch, lax.rem(x + d, 4))]
            remote(piece, piece, x2s.at[ch, d], x2r.at[ch, d], xs[d]).wait_recv()
        count = SIZES[ch] * rows
        got = refkv[STARTS[ch] * rows:STARTS[ch] * rows + count, :]
        base = (16 + STARTS[ch]) * rows
        kt[:HEAD, base:base + count] = got[:, :HEAD].astype(jnp.float32).T.astype(jnp.bfloat16)
        va[base:base + count, :HEAD] = got[:, HEAD:]

    def block(b):
        return slice(b * QROWS, (b + 1) * QROWS)

    def scores(b, keys, slot):
        k0, k1 = keys
        qt = q[block(b), :]
        top = None
        for k in range(k0, k1, KSTEP):
            score = jnp.dot(qt, kt[:, k:k + KSTEP], preferred_element_type=jnp.float32)
            s[slot, :, k - k0:k - k0 + KSTEP] = score
            for m in range(KSTEP // 128):
                piece = score[:, m * 128:(m + 1) * 128]
                top = piece if top is None else jnp.maximum(top, piece)
        return jnp.broadcast_to(jnp.max(top, axis=1, keepdims=True), (QROWS, 128))

    def mix(b, keys, slot, top, fresh):
        k0, k1 = keys
        acc = None
        if not fresh:
            old = top_all[block(b), :]
            top = jnp.maximum(top, old)
            shrink = jnp.exp2(old - top)
            acc = jnp.concatenate([acc_all[block(b), :HEAD] * shrink, acc_all[block(b), HEAD:] * shrink], axis=1)
        top_all[block(b), :] = top
        wide = jnp.concatenate([top] * (KSTEP // 128), axis=1)
        for k in range(k0, k1, KSTEP):
            weight = jnp.exp2((s[slot, :, k - k0:k - k0 + KSTEP] - wide).astype(jnp.bfloat16))
            more = jnp.dot(weight, va[k:k + KSTEP, :], preferred_element_type=jnp.float32)
            acc = more if acc is None else acc + more
        return acc

    def attend(blocks, keys, fresh=False, done=None):
        tops = [scores(blocks[0], keys, 0)]
        for n, b in enumerate(blocks):
            if n + 1 < len(blocks):
                tops.append(scores(blocks[n + 1], keys, (n + 1) % 2))
            acc = mix(b, keys, n % 2, tops[n], fresh)
            if done is None:
                acc_all[block(b), :] = acc
            else:
                done(b, acc)

    def my_columns():
        return pl.ds(pl.multiple_of(me * HEAD, HEAD), HEAD)

    def o_copy(j):
        place_there = (j // 8) * 8 + MIRROR[j % 8]
        return remote(mixed.at[j], out.at[:, my_columns()], os.at[j], orv.at[place_there], owners[j])

    def finish(b, acc):
        result = (acc[:, :HEAD] / acc[:, HEAD:HEAD + 1]).astype(jnp.bfloat16)
        for n in range(QROWS // TILE):
            j = b * (QROWS // TILE) + n
            if j == 0:
                out[:, my_columns()] = result[:TILE]
            else:
                mixed[j] = result[n * TILE:(n + 1) * TILE]
                go(o_copy(j))

    local[0].wait()
    for k in (0, 2, 1, 3):
        go(z1_copy(k))
    for j in range(4):
        go(y_copy(0, CW, j))
        go(y_copy(0, CCW, (2, 3, 0, 1)[j]))
    for k in range(PIECES):
        go(s_copy(0, 0, k))

    tiles = mask.shape[0]
    tile_row = lax.broadcasted_iota(jnp.int32, (tiles, 2 * tiles), 0)
    tile_col = lax.broadcasted_iota(jnp.int32, (tiles, 2 * tiles), 1)
    allow = jnp.where((mask[...] == 1) | (tile_row == tile_col), 1.0, 0.0).astype(jnp.bfloat16)

    def order_of(tile):
        far = jnp.where(lax.div(tile, 8) == zh, 0, 8)
        dy = lax.rem(lax.rem(lax.div(tile, 2), 4) + 4 - y, 4)
        o = jnp.where(lax.rem(tile, 2) == c, 0, 1)
        near = jnp.where(dy == 0, o, jnp.where(dy == 2, 6 + o, jnp.where(dy == 3, 2, 3) + 2 * o))
        return far + near

    turn = jnp.where(
        order_of(lax.broadcasted_iota(jnp.int32, (tiles, tiles), 1)) == lax.broadcasted_iota(jnp.int32, (tiles, tiles), 0),
        1.0, 0.0).astype(jnp.bfloat16)
    turned = jnp.dot(turn, allow, preferred_element_type=jnp.float32).astype(jnp.bfloat16)
    spread_shape = (tiles, tiles * TILE)
    spread = jnp.where(
        order_of(lax.broadcasted_iota(jnp.int32, spread_shape, 0)) == lax.div(lax.broadcasted_iota(jnp.int32, spread_shape, 1), TILE),
        1.0, 0.0).astype(jnp.bfloat16)
    for side in range(2):
        wide = jnp.dot(turned[:, side * tiles:(side + 1) * tiles], spread, preferred_element_type=jnp.float32)
        kt[HEAD:HEAD + tiles, side * tiles * TILE:(side + 1) * tiles * TILE] = jnp.where(wide > 0.5, 0.0, LOW).astype(jnp.bfloat16)
    kt[HEAD + tiles:, :] = jnp.zeros((HEAD - tiles, 2 * tiles * TILE), jnp.bfloat16)
    va[:, HEAD:] = jnp.ones((2 * tiles * TILE, HEAD), jnp.bfloat16)

    for copy in local[1:]:
        copy.wait()
    project(0)
    take_y(0, CW, 0)
    take_y(0, CCW, 2)
    project(1)
    keys_send(0)
    relay_on(0)
    relay_on(2)
    take_y(0, CW, 1)
    take_y(0, CCW, 3)
    take_y(0, CW, 2)
    take_y(0, CCW, 0)
    relay_on(1)
    relay_on(3)
    take_y(0, CW, 3)
    take_y(0, CCW, 1)
    project(2)
    project(3)
    keys_send(1)
    take_z(0)
    take_z(2)
    keys_step(0)
    project(4)
    project(5)
    keys_send(2)
    take_y(0, CW, 4)
    take_y(0, CCW, 4)
    take_y(0, CW, 5)
    take_y(0, CCW, 5)
    take_y(1, CW, 0)
    take_y(1, CCW, 2)
    keys_step(1)
    project(6)
    take_z(1)
    take_z(3)
    keys_step(2)
    project(8)
    take_y(1, CW, 2)
    take_y(1, CCW, 0)
    project(7)
    keys_send(3)
    project(9)
    keys_send(4)
    keys_step(3)
    take_y(1, CW, 1)
    take_y(1, CCW, 3)
    keys_step(4)
    attend((0, 1), OWN0, True)
    take_y(1, CW, 4)
    take_y(1, CCW, 4)
    take_y(1, CW, 3)
    take_y(1, CCW, 1)
    project(10)
    project(11)
    keys_send(5)
    take_y(1, CW, 5)
    take_y(1, CCW, 5)
    keys_step(5)
    project(12)
    project(13)
    keys_send(6)
    project(14)
    keys_send(7)
    keys_step(6)
    project(15)
    keys_send(8)
    keys_step(7)
    attend((2, 3), OWN0, True)
    keys_step(8)
    attend((0, 1), OWN1)
    keys_step(9)
    keys_step(10)
    attend((2, 3), OWN1)
    keys_step(11)
    for ch in range(4):
        keys_take(ch)
    keys_step(12)
    attend((0, 1), REF0)
    keys_step(13)
    keys_step(14)
    attend((2, 3), REF0)
    for ch in (4, 5, 6):
        keys_take(ch)
    attend((0, 1, 2, 3), REF1)
    for ch in (7, 8):
        keys_take(ch)
    attend((2, 3, 0, 1), LAST, done=finish)
    for j in range(1, 16):
        f, dy, cc = logical(j)
        there = out.at[:, pl.ds(pl.multiple_of(shard(f, dy, cc) * HEAD, HEAD), HEAD)]
        remote(there, there, os.at[j], orv.at[j], owners[j]).wait_recv()
    for copy in started:
        copy.wait_send()

    @pl.when(zl < 3)
    def _():
        for ch in range(CHUNKS):
            r_copy(ch).wait_send()

    @pl.when(zl > 0)
    def _():
        for ch in range(CHUNKS):
            l_copy(ch).wait_send()


def whole_block(references, pairing, mask, bias, tok, w, down, up):
    rows, width = tok.shape
    length = 16 * rows
    dma = pltpu.SemaphoreType.DMA
    vmem = pl.BlockSpec(memory_space=pltpu.VMEM)
    smem = pl.BlockSpec(memory_space=pltpu.SMEM)
    anywhere = pl.BlockSpec(memory_space=pl.ANY)
    half = jnp.bfloat16
    pieces = pltpu.VMEM((CHUNKS, 4, rows // 2, 2 * HEAD), half)
    return pl.pallas_call(
        block_kernel,
        out_shape=jax.ShapeDtypeStruct((rows, 16 * HEAD), half),
        in_specs=[smem, smem, vmem, vmem] + [anywhere] * 4,
        out_specs=vmem,
        scratch_shapes=[
            pltpu.VMEM((16, rows, width), half),
            pltpu.VMEM((PIECES, rows // PIECES, width), half),
            pltpu.VMEM(w.shape, half),
            pltpu.VMEM(down.shape, half),
            pltpu.VMEM(up.shape, half),
            pltpu.VMEM((length, 2 * HEAD), half),
            pltpu.VMEM((2 * HEAD, 2 * length), half),
            pltpu.VMEM((2 * length, 2 * HEAD), half),
            pltpu.VMEM((length, 2 * HEAD), half),
            pltpu.VMEM((length, 2 * HEAD), half),
            pieces, pieces, pieces, pieces, pieces, pieces, pieces,
            pltpu.VMEM((2, QROWS, KROWS), jnp.float32),
            pltpu.VMEM((length, 128), jnp.float32),
            pltpu.VMEM((length, 2 * HEAD), jnp.float32),
            pltpu.VMEM((16, rows, HEAD), half),
            dma((4,)),
            dma((4,)), dma((4,)), dma((4,)), dma((4,)),
            dma((2, 2, 6)), dma((2, 2, 6)),
            dma((2, 4, 4)), dma((2, 4, 4)),
            dma((CHUNKS, 4)), dma((CHUNKS, 4)),
            dma((CHUNKS,)), dma((CHUNKS,)), dma((CHUNKS,)), dma((CHUNKS,)),
            dma((CHUNKS, 4)), dma((CHUNKS, 4)),
            dma((16,)), dma((16,)),
        ],
        compiler_params=pltpu.CompilerParams(
            collective_id=0, has_side_effects=True, vmem_limit_bytes=56 * 2**20),
        name="attention_block",
    )(references, pairing, mask, bias, tok, w, down, up)


def on_device(tokens, projection_weight, projection_bias, adapter_down_weight, adapter_up_weight,
              tile_allow_mask, references, pairing):
    return whole_block(references, pairing, tile_allow_mask[0], projection_bias, tokens[0],
                       projection_weight[:, 0], adapter_down_weight[0].T, adapter_up_weight[0, :, 0])[None]


def solution(mesh):
    in_specs = (
        P("req", "patch", None),
        P(None, "patch", None),
        P("patch", None),
        P("req", None, None),
        P("req", None, "patch", None),
        P("req", None, None),
        P(),
        P(),
    )
    return jax.shard_map(
        on_device, mesh=mesh, in_specs=in_specs, out_specs=P("req", "patch", None), check_vma=False
    )
```

```python
import math

import jax
import jax.numpy as jnp
from jax import lax
from jax.experimental import pallas as pl
from jax.experimental.pallas import tpu as pltpu
from jax.sharding import PartitionSpec as P

MESH = pl.DeviceIdType.MESH
CW, CCW = 0, 1
PIECES = 4
HALVES = ((0, 1), (2, 3))
TILE = 128
HEAD = 128
SIZES = (2, 2, 2, 2, 2, 2, 1, 1, 1, 1)
STARTS = tuple(sum(SIZES[:n]) for n in range(len(SIZES)))
CHUNKS = len(SIZES)
LAG = 2
QROWS = 512
KROWS = 1024
KSTEP = 256
LOW = -1e30
OWN0, OWN1, REF0, REF1, LAST = (0, 1024), (1024, 2048), (2048, 3072), (3072, 3840), (3840, 4096)
QSCALE = math.log2(math.e) / math.sqrt(HEAD)
ORDER = ((0, 0), (0, 1), (3, 0), (1, 0), (3, 1), (1, 1), (2, 0), (2, 1))
MIRROR = (0, 1, 3, 2, 5, 4, 6, 7)


def place():
    r, p = lax.axis_index("req"), lax.axis_index("patch")
    return lax.div(r, 4), lax.rem(r, 4), lax.div(p, 8), lax.rem(lax.div(p, 2), 4), lax.rem(p, 2)


def at(x, z, y, c):
    z = lax.rem(z, 8)
    return (lax.rem(x, 4) * 4 + lax.rem(z, 4), lax.div(z, 4) * 8 + lax.rem(y, 4) * 2 + c)


def pick(values, index):
    out = values[0]
    for n in range(1, len(values)):
        out = jnp.where(index == n, values[n], out)
    return out


def block_kernel(references, pairing, mask, bias, tok_hbm, w_hbm, down_hbm, up_hbm, out,
                 held, relay, w, down, up, q, kt, va, kv, refkv, xin, chosen, rs, rr, ls, lr, xout,
                 s, top_all, acc_all, mixed,
                 lsem, z1s, z1r, z2s, z2r, ys, yr, ss, sr,
                 x1s, x1r, rsend, rrecv, lsend, lrecv, x2s, x2r, os, orv):
    x, zl, zh, y, c = place()
    z = zh * 4 + zl
    rows = tok_hbm.shape[0]
    step = rows // PIECES
    quarter = rows // 4
    other = 1 - c
    me = zh * 8 + y * 2 + c

    def shard(f, dy, cc):
        half = zh if f == 0 else 1 - zh
        return half * 8 + lax.rem(y + dy, 4) * 2 + cc

    def logical(j):
        f, (dy, o) = j // 8, ORDER[j % 8]
        return f, dy, (other if o else c)

    tok = held.at[me]
    local = [
        pltpu.make_async_copy(tok_hbm, tok, lsem.at[0]),
        pltpu.make_async_copy(w_hbm, w, lsem.at[1]),
        pltpu.make_async_copy(down_hbm, down, lsem.at[2]),
        pltpu.make_async_copy(up_hbm, up, lsem.at[3]),
    ]
    for copy in local:
        copy.start()

    sibling = at(x, z, y, other)
    ring = (at(x, z, y + 1, c), at(x, z, y + 3, c))
    zring = (at(x, z + 2, y, c), at(x, z + 6, y, c))
    xs = [at(x + d, z, y, c) for d in range(4)]
    right = at(x, zh * 4 + lax.rem(zl + 1, 4), y, c)
    left = at(x, zh * 4 + lax.rem(zl + 3, 4), y, c)
    owners = []
    for j in range(16):
        f, dy, cc = logical(j)
        owners.append((x * 4 + zl, shard(f, dy, cc)))

    barrier = pltpu.get_barrier_semaphore()
    everyone = (sibling, *ring, *zring, *xs[1:], right, left)
    for who in everyone:
        pl.semaphore_signal(barrier, inc=1, device_id=who, device_id_type=MESH)
    pl.semaphore_wait(barrier, len(everyone))

    def remote(src, dst, send, recv, who):
        return pltpu.make_async_remote_copy(
            src_ref=src, dst_ref=dst, send_sem=send, recv_sem=recv, device_id=who, device_id_type=MESH)

    started = []

    def go(copy):
        copy.start()
        started.append(copy)

    def span(k):
        return pl.ds(k * step, step)

    def y_copy(f, way, j):
        if j < 4:
            p, k = shard(f, 0, c), j
        else:
            p, k = shard(f, 3 if way == CW else 1, c), HALVES[way][j - 4]
        piece = held.at[p, span(k)]
        return remote(piece, piece, ys.at[f, way, j], yr.at[f, way, j], ring[way])

    def y_arrived(f, way, j):
        if j < 4:
            p, k = shard(f, 3 if way == CW else 1, c), j
        else:
            p, k = shard(f, 2, c), HALVES[way][j - 4]
        piece = held.at[p, span(k)]
        remote(piece, piece, ys.at[f, way, j], yr.at[f, way, j], ring[way]).wait_recv()

    def s_copy(f, dy, k):
        piece = held.at[shard(f, dy, c), span(k)]
        return remote(piece, piece, ss.at[f, dy, k], sr.at[f, dy, k], sibling)

    def s_arrived(f, dy, k):
        piece = held.at[shard(f, dy, other), span(k)]
        remote(piece, piece, ss.at[f, dy, k], sr.at[f, dy, k], sibling).wait_recv()

    def z1_copy(k):
        return remote(tok.at[span(k)], relay.at[k], z1s.at[k], z1r.at[k], zring[0 if k < 2 else 1])

    def z2_copy(k):
        way = 0 if k < 2 else 1
        oz = lax.rem(z + (6 if way == 0 else 2), 8)
        p = lax.div(oz, 4) * 8 + y * 2 + c
        return remote(relay.at[k], held.at[p, span(k)], z2s.at[k], z2r.at[k], zring[way])

    def take_y(f, way, j):
        y_arrived(f, way, j)
        if j < 4:
            if j in HALVES[way]:
                go(y_copy(f, way, 4 + HALVES[way].index(j)))
            go(s_copy(f, 3 if way == CW else 1, j))
        else:
            go(s_copy(f, 2, HALVES[way][j - 4]))

    def relay_on(k):
        remote(relay.at[k], relay.at[k], z1s.at[k], z1r.at[k], sibling).wait_recv()
        go(z2_copy(k))

    def take_z(k):
        piece = held.at[shard(1, 0, c), span(k)]
        remote(piece, piece, z2s.at[k], z2r.at[k], sibling).wait_recv()
        go(y_copy(1, CW, k))
        go(y_copy(1, CCW, k))
        go(s_copy(1, 0, k))

    def project(j):
        f, dy, cc = logical(j)
        if ORDER[j % 8][1]:
            for k in range(PIECES):
                s_arrived(f, dy, k)
        t = held[shard(f, dy, cc)]
        low = lax.dot_general(t, down[...], (((1,), (1,)), ((), ())), preferred_element_type=jnp.float32)
        acc = jnp.dot(t, w[...], preferred_element_type=jnp.float32)
        acc = acc + jnp.dot(low.astype(jnp.bfloat16), up[...], preferred_element_type=jnp.float32)
        acc = acc + bias[...].astype(jnp.float32)
        here = slice(j * rows, (j + 1) * rows)
        q[here, :HEAD] = (acc[:, :HEAD] * QSCALE).astype(jnp.bfloat16)
        column = lax.broadcasted_iota(jnp.int32, (rows, HEAD), 1)
        q[here, HEAD:] = jnp.where(column == j, 1.0, 0.0).astype(jnp.bfloat16)
        kv[here, :] = acc[:, HEAD:].astype(jnp.bfloat16)
        kt[:HEAD, here] = acc[:, HEAD:2 * HEAD].T.astype(jnp.bfloat16)
        va[here, :HEAD] = acc[:, 2 * HEAD:].astype(jnp.bfloat16)

    def size(ch):
        return SIZES[ch] * quarter

    def piece_rows(ch, n):
        return pl.ds(pl.multiple_of(STARTS[ch] * rows + n * size(ch), quarter), size(ch))

    def first(ch):
        return pl.ds(0, size(ch))

    def x1_copy(ch, d):
        return remote(kv.at[piece_rows(ch, lax.rem(x + d, 4))], xin.at[ch, x, first(ch)],
                      x1s.at[ch, d], x1r.at[ch, 4 - d], xs[d])

    def x2_copy(ch, d):
        return remote(xout.at[ch, d, first(ch)], refkv.at[piece_rows(ch, x)],
                      x2s.at[ch, d], x2r.at[ch, 4 - d], xs[d])

    def r_copy(ch):
        return remote(rs.at[ch, :, first(ch)], rr.at[ch, :, first(ch)], rsend.at[ch], rrecv.at[ch], right)

    def l_copy(ch):
        return remote(ls.at[ch, :, first(ch)], lr.at[ch, :, first(ch)], lsend.at[ch], lrecv.at[ch], left)

    columns = [lax.div(references[n], 4) for n in range(4)]
    planes = [lax.rem(references[n], 4) for n in range(4)]
    slots = [pairing[lax.rem(x + d, 4) * 4 + zl] for d in range(4)]

    def keys_send(ch):
        for d in (2, 1, 3):
            go(x1_copy(ch, d))
        xin[ch, x, first(ch)] = kv[piece_rows(ch, x), :]

    def is_mine(slot):
        return planes[slot] == zl

    def flow(ch, copy, incoming, outgoing, source, sink):
        if source:
            piece = incoming.at[ch, :, first(ch)]
            if incoming is rr:
                remote(piece, piece, rsend.at[ch], rrecv.at[ch], left).wait_recv()
            else:
                remote(piece, piece, lsend.at[ch], lrecv.at[ch], right).wait_recv()
        if sink:
            for slot in range(4):
                value = chosen[ch, slot, first(ch)]
                if source:
                    value = jnp.where(is_mine(slot), value, incoming[ch, slot, first(ch)])
                outgoing[ch, slot, first(ch)] = value
            copy(ch).start()

    def keys_step(t):
        if t < CHUNKS:
            for d in (1, 3, 2):
                piece = xin.at[t, lax.rem(x + d, 4), first(t)]
                remote(piece, piece, x1s.at[t, d], x1r.at[t, d], xs[d]).wait_recv()
            here = [xin[t, n, first(t)] for n in range(4)]
            for slot in range(4):
                chosen[t, slot, first(t)] = pick(here, columns[slot])

        for line in range(4):
            rc, lc = t - LAG * line, t - LAG * (3 - line)

            @pl.when(zl == line)
            def _():
                def rightward():
                    if 0 <= rc < CHUNKS:
                        flow(rc, r_copy, rr, rs, line > 0, line < 3)

                def leftward():
                    if 0 <= lc < CHUNKS:
                        flow(lc, l_copy, lr, ls, line < 3, line > 0)

                if line < 2:
                    rightward()
                    leftward()
                else:
                    leftward()
                    rightward()

        ch = t - 3 * LAG
        if 0 <= ch < CHUNKS:
            final = []
            for slot in range(4):
                far = jnp.where(planes[slot] < zl, rr[ch, slot, first(ch)], lr[ch, slot, first(ch)])
                final.append(jnp.where(is_mine(slot), chosen[ch, slot, first(ch)], far))
            for d in (2, 1, 3):
                xout[ch, d, first(ch)] = pick(final, slots[d])
                go(x2_copy(ch, d))
            refkv[piece_rows(ch, x), :] = pick(final, slots[0])

    def keys_take(ch):
        for d in (1, 3, 2):
            piece = refkv.at[piece_rows(ch, lax.rem(x + d, 4))]
            remote(piece, piece, x2s.at[ch, d], x2r.at[ch, d], xs[d]).wait_recv()
        count = SIZES[ch] * rows
        got = refkv[STARTS[ch] * rows:STARTS[ch] * rows + count, :]
        base = (16 + STARTS[ch]) * rows
        kt[:HEAD, base:base + count] = got[:, :HEAD].astype(jnp.float32).T.astype(jnp.bfloat16)
        va[base:base + count, :HEAD] = got[:, HEAD:]

    def block(b):
        return slice(b * QROWS, (b + 1) * QROWS)

    def scores(b, keys, slot):
        k0, k1 = keys
        qt = q[block(b), :]
        top = None
        for k in range(k0, k1, KSTEP):
            score = jnp.dot(qt, kt[:, k:k + KSTEP], preferred_element_type=jnp.float32)
            s[slot, :, k - k0:k - k0 + KSTEP] = score
            for m in range(KSTEP // 128):
                piece = score[:, m * 128:(m + 1) * 128]
                top = piece if top is None else jnp.maximum(top, piece)
        return jnp.broadcast_to(jnp.max(top, axis=1, keepdims=True), (QROWS, 128))

    def mix(b, keys, slot, top, fresh):
        k0, k1 = keys
        acc = None
        if not fresh:
            old = top_all[block(b), :]
            top = jnp.maximum(top, old)
            shrink = jnp.exp2(old - top)
            acc = jnp.concatenate([acc_all[block(b), :HEAD] * shrink, acc_all[block(b), HEAD:] * shrink], axis=1)
        top_all[block(b), :] = top
        wide = jnp.concatenate([top] * (KSTEP // 128), axis=1)
        for k in range(k0, k1, KSTEP):
            weight = jnp.exp2((s[slot, :, k - k0:k - k0 + KSTEP] - wide).astype(jnp.bfloat16))
            more = jnp.dot(weight, va[k:k + KSTEP, :], preferred_element_type=jnp.float32)
            acc = more if acc is None else acc + more
        return acc

    def attend(blocks, keys, fresh=False, done=None):
        tops = [scores(blocks[0], keys, 0)]
        for n, b in enumerate(blocks):
            if n + 1 < len(blocks):
                tops.append(scores(blocks[n + 1], keys, (n + 1) % 2))
            acc = mix(b, keys, n % 2, tops[n], fresh)
            if done is None:
                acc_all[block(b), :] = acc
            else:
                done(b, acc)

    def my_columns():
        return pl.ds(pl.multiple_of(me * HEAD, HEAD), HEAD)

    def o_copy(j):
        place_there = (j // 8) * 8 + MIRROR[j % 8]
        return remote(mixed.at[j], out.at[:, my_columns()], os.at[j], orv.at[place_there], owners[j])

    def finish(b, acc):
        result = (acc[:, :HEAD] / acc[:, HEAD:HEAD + 1]).astype(jnp.bfloat16)
        for n in range(QROWS // TILE):
            j = b * (QROWS // TILE) + n
            if j == 0:
                out[:, my_columns()] = result[:TILE]
            else:
                mixed[j] = result[n * TILE:(n + 1) * TILE]
                go(o_copy(j))

    local[0].wait()
    for k in (0, 2, 1, 3):
        go(z1_copy(k))
    for j in range(4):
        go(y_copy(0, CW, j))
        go(y_copy(0, CCW, (2, 3, 0, 1)[j]))
    for k in range(PIECES):
        go(s_copy(0, 0, k))

    tiles = mask.shape[0]
    tile_row = lax.broadcasted_iota(jnp.int32, (tiles, 2 * tiles), 0)
    tile_col = lax.broadcasted_iota(jnp.int32, (tiles, 2 * tiles), 1)
    allow = jnp.where((mask[...] == 1) | (tile_row == tile_col), 1.0, 0.0).astype(jnp.bfloat16)

    def order_of(tile):
        far = jnp.where(lax.div(tile, 8) == zh, 0, 8)
        dy = lax.rem(lax.rem(lax.div(tile, 2), 4) + 4 - y, 4)
        o = jnp.where(lax.rem(tile, 2) == c, 0, 1)
        near = jnp.where(dy == 0, o, jnp.where(dy == 2, 6 + o, jnp.where(dy == 3, 2, 3) + 2 * o))
        return far + near

    turn = jnp.where(
        order_of(lax.broadcasted_iota(jnp.int32, (tiles, tiles), 1)) == lax.broadcasted_iota(jnp.int32, (tiles, tiles), 0),
        1.0, 0.0).astype(jnp.bfloat16)
    turned = jnp.dot(turn, allow, preferred_element_type=jnp.float32).astype(jnp.bfloat16)
    spread_shape = (tiles, tiles * TILE)
    spread = jnp.where(
        order_of(lax.broadcasted_iota(jnp.int32, spread_shape, 0)) == lax.div(lax.broadcasted_iota(jnp.int32, spread_shape, 1), TILE),
        1.0, 0.0).astype(jnp.bfloat16)
    for side in range(2):
        wide = jnp.dot(turned[:, side * tiles:(side + 1) * tiles], spread, preferred_element_type=jnp.float32)
        kt[HEAD:HEAD + tiles, side * tiles * TILE:(side + 1) * tiles * TILE] = jnp.where(wide > 0.5, 0.0, LOW).astype(jnp.bfloat16)
    kt[HEAD + tiles:, :] = jnp.zeros((HEAD - tiles, 2 * tiles * TILE), jnp.bfloat16)
    va[:, HEAD:] = jnp.ones((2 * tiles * TILE, HEAD), jnp.bfloat16)

    for copy in local[1:]:
        copy.wait()
    project(0)
    take_y(0, CW, 0)
    take_y(0, CCW, 2)
    project(1)
    keys_send(0)
    relay_on(0)
    relay_on(2)
    take_y(0, CW, 1)
    take_y(0, CCW, 3)
    take_y(0, CW, 2)
    take_y(0, CCW, 0)
    relay_on(1)
    relay_on(3)
    take_y(0, CW, 3)
    take_y(0, CCW, 1)
    project(2)
    project(3)
    keys_send(1)
    take_z(0)
    take_z(2)
    keys_step(0)
    project(4)
    project(5)
    keys_send(2)
    take_y(0, CW, 4)
    take_y(0, CCW, 4)
    take_y(0, CW, 5)
    take_y(0, CCW, 5)
    take_y(1, CW, 0)
    take_y(1, CCW, 2)
    keys_step(1)
    project(6)
    take_z(1)
    take_z(3)
    keys_step(2)
    project(8)
    take_y(1, CW, 2)
    take_y(1, CCW, 0)
    project(7)
    keys_send(3)
    project(9)
    keys_send(4)
    keys_step(3)
    take_y(1, CW, 1)
    take_y(1, CCW, 3)
    keys_step(4)
    attend((0, 1), OWN0, True)
    take_y(1, CW, 4)
    take_y(1, CCW, 4)
    take_y(1, CW, 3)
    take_y(1, CCW, 1)
    project(10)
    project(11)
    keys_send(5)
    take_y(1, CW, 5)
    take_y(1, CCW, 5)
    keys_step(5)
    project(12)
    keys_send(6)
    project(13)
    keys_send(7)
    keys_step(6)
    project(14)
    keys_send(8)
    keys_step(7)
    project(15)
    keys_send(9)
    keys_step(8)
    attend((2, 3), OWN0, True)
    keys_step(9)
    keys_step(10)
    attend((0, 1), OWN1)
    keys_step(11)
    keys_step(12)
    attend((2, 3), OWN1)
    keys_step(13)
    for ch in range(4):
        keys_take(ch)
    keys_step(14)
    keys_step(15)
    attend((0, 1), REF0)
    attend((2, 3), REF0)
    for ch in (4, 5, 6, 7):
        keys_take(ch)
    attend((0, 1, 2, 3), REF1)
    for ch in (8, 9):
        keys_take(ch)
    attend((2, 3, 0, 1), LAST, done=finish)
    for copy in started:
        copy.wait_send()

    @pl.when(zl < 3)
    def _():
        for ch in range(CHUNKS):
            r_copy(ch).wait_send()

    @pl.when(zl > 0)
    def _():
        for ch in range(CHUNKS):
            l_copy(ch).wait_send()

    for j in range(1, 16):
        f, dy, cc = logical(j)
        there = out.at[:, pl.ds(pl.multiple_of(shard(f, dy, cc) * HEAD, HEAD), HEAD)]
        remote(there, there, os.at[j], orv.at[j], owners[j]).wait_recv()


def whole_block(references, pairing, mask, bias, tok, w, down, up):
    rows, width = tok.shape
    length = 16 * rows
    dma = pltpu.SemaphoreType.DMA
    vmem = pl.BlockSpec(memory_space=pltpu.VMEM)
    smem = pl.BlockSpec(memory_space=pltpu.SMEM)
    anywhere = pl.BlockSpec(memory_space=pl.ANY)
    half = jnp.bfloat16
    pieces = pltpu.VMEM((CHUNKS, 4, rows // 2, 2 * HEAD), half)
    return pl.pallas_call(
        block_kernel,
        out_shape=jax.ShapeDtypeStruct((rows, 16 * HEAD), half),
        in_specs=[smem, smem, vmem, vmem] + [anywhere] * 4,
        out_specs=vmem,
        scratch_shapes=[
            pltpu.VMEM((16, rows, width), half),
            pltpu.VMEM((PIECES, rows // PIECES, width), half),
            pltpu.VMEM(w.shape, half),
            pltpu.VMEM(down.shape, half),
            pltpu.VMEM(up.shape, half),
            pltpu.VMEM((length, 2 * HEAD), half),
            pltpu.VMEM((2 * HEAD, 2 * length), half),
            pltpu.VMEM((2 * length, 2 * HEAD), half),
            pltpu.VMEM((length, 2 * HEAD), half),
            pltpu.VMEM((length, 2 * HEAD), half),
            pieces, pieces, pieces, pieces, pieces, pieces, pieces,
            pltpu.VMEM((2, QROWS, KROWS), jnp.float32),
            pltpu.VMEM((length, 128), jnp.float32),
            pltpu.VMEM((length, 2 * HEAD), jnp.float32),
            pltpu.VMEM((16, rows, HEAD), half),
            dma((4,)),
            dma((4,)), dma((4,)), dma((4,)), dma((4,)),
            dma((2, 2, 6)), dma((2, 2, 6)),
            dma((2, 4, 4)), dma((2, 4, 4)),
            dma((CHUNKS, 4)), dma((CHUNKS, 4)),
            dma((CHUNKS,)), dma((CHUNKS,)), dma((CHUNKS,)), dma((CHUNKS,)),
            dma((CHUNKS, 4)), dma((CHUNKS, 4)),
            dma((16,)), dma((16,)),
        ],
        compiler_params=pltpu.CompilerParams(
            collective_id=0, has_side_effects=True, vmem_limit_bytes=56 * 2**20),
        name="attention_block",
    )(references, pairing, mask, bias, tok, w, down, up)


def on_device(tokens, projection_weight, projection_bias, adapter_down_weight, adapter_up_weight,
              tile_allow_mask, references, pairing):
    return whole_block(references, pairing, tile_allow_mask[0], projection_bias, tokens[0],
                       projection_weight[:, 0], adapter_down_weight[0].T, adapter_up_weight[0, :, 0])[None]


def solution(mesh):
    in_specs = (
        P("req", "patch", None),
        P(None, "patch", None),
        P("patch", None),
        P("req", None, None),
        P("req", None, "patch", None),
        P("req", None, None),
        P(),
        P(),
    )
    return jax.shard_map(
        on_device, mesh=mesh, in_specs=in_specs, out_specs=P("req", "patch", None), check_vma=False
    )
```

```python
import math

import jax
import jax.numpy as jnp
from jax import lax
from jax.experimental import pallas as pl
from jax.experimental.pallas import tpu as pltpu
from jax.sharding import PartitionSpec as P

MESH = pl.DeviceIdType.MESH
CW, CCW = 0, 1
PIECES = 4
HALVES = ((0, 1), (2, 3))
TILE = 128
HEAD = 128
SIZES = (2, 2, 2, 2, 2, 2, 1, 1, 1, 1)
STARTS = tuple(sum(SIZES[:n]) for n in range(len(SIZES)))
CHUNKS = len(SIZES)
LAG = 2
QROWS = 512
KROWS = 1024
KSTEP = 256
LOW = -1e30
OWN0, OWN1, REF0, REF1, LAST = (0, 1024), (1024, 2048), (2048, 3072), (3072, 3840), (3840, 4096)
QSCALE = math.log2(math.e) / math.sqrt(HEAD)
ORDER = ((0, 0), (0, 1), (3, 0), (1, 0), (3, 1), (1, 1), (2, 0), (2, 1))
MIRROR = (0, 1, 3, 2, 5, 4, 6, 7)


def place():
    r, p = lax.axis_index("req"), lax.axis_index("patch")
    return lax.div(r, 4), lax.rem(r, 4), lax.div(p, 8), lax.rem(lax.div(p, 2), 4), lax.rem(p, 2)


def at(x, z, y, c):
    z = lax.rem(z, 8)
    return (lax.rem(x, 4) * 4 + lax.rem(z, 4), lax.div(z, 4) * 8 + lax.rem(y, 4) * 2 + c)


def pick(values, index):
    out = values[0]
    for n in range(1, len(values)):
        out = jnp.where(index == n, values[n], out)
    return out


def block_kernel(references, pairing, mask, bias, tok_hbm, w_hbm, down_hbm, up_hbm, out,
                 held, relay, w, down, up, q, kt, va, kv, refkv, xin, chosen, rs, rr, ls, lr, xout,
                 s, top_all, acc_all, mixed,
                 lsem, z1s, z1r, z2s, z2r, ys, yr, ss, sr,
                 x1s, x1r, rsend, rrecv, lsend, lrecv, x2s, x2r, os, orv):
    x, zl, zh, y, c = place()
    z = zh * 4 + zl
    rows = tok_hbm.shape[0]
    step = rows // PIECES
    quarter = rows // 4
    other = 1 - c
    me = zh * 8 + y * 2 + c

    def shard(f, dy, cc):
        half = zh if f == 0 else 1 - zh
        return half * 8 + lax.rem(y + dy, 4) * 2 + cc

    def logical(j):
        f, (dy, o) = j // 8, ORDER[j % 8]
        return f, dy, (other if o else c)

    tok = held.at[me]
    local = [
        pltpu.make_async_copy(tok_hbm, tok, lsem.at[0]),
        pltpu.make_async_copy(w_hbm, w, lsem.at[1]),
        pltpu.make_async_copy(down_hbm, down, lsem.at[2]),
        pltpu.make_async_copy(up_hbm, up, lsem.at[3]),
    ]
    for copy in local:
        copy.start()

    sibling = at(x, z, y, other)
    ring = (at(x, z, y + 1, c), at(x, z, y + 3, c))
    zring = (at(x, z + 2, y, c), at(x, z + 6, y, c))
    xs = [at(x + d, z, y, c) for d in range(4)]
    right = at(x, zh * 4 + lax.rem(zl + 1, 4), y, c)
    left = at(x, zh * 4 + lax.rem(zl + 3, 4), y, c)
    owners = []
    for j in range(16):
        f, dy, cc = logical(j)
        owners.append((x * 4 + zl, shard(f, dy, cc)))

    barrier = pltpu.get_barrier_semaphore()
    everyone = (sibling, *ring, *zring, *xs[1:], right, left)
    for who in everyone:
        pl.semaphore_signal(barrier, inc=1, device_id=who, device_id_type=MESH)
    pl.semaphore_wait(barrier, len(everyone))

    def remote(src, dst, send, recv, who):
        return pltpu.make_async_remote_copy(
            src_ref=src, dst_ref=dst, send_sem=send, recv_sem=recv, device_id=who, device_id_type=MESH)

    started = []

    def go(copy):
        copy.start()
        started.append(copy)

    def span(k):
        return pl.ds(k * step, step)

    def y_copy(f, way, j):
        if j < 4:
            p, k = shard(f, 0, c), j
        else:
            p, k = shard(f, 3 if way == CW else 1, c), HALVES[way][j - 4]
        piece = held.at[p, span(k)]
        return remote(piece, piece, ys.at[f, way, j], yr.at[f, way, j], ring[way])

    def y_arrived(f, way, j):
        if j < 4:
            p, k = shard(f, 3 if way == CW else 1, c), j
        else:
            p, k = shard(f, 2, c), HALVES[way][j - 4]
        piece = held.at[p, span(k)]
        remote(piece, piece, ys.at[f, way, j], yr.at[f, way, j], ring[way]).wait_recv()

    def s_copy(f, dy, k):
        piece = held.at[shard(f, dy, c), span(k)]
        return remote(piece, piece, ss.at[f, dy, k], sr.at[f, dy, k], sibling)

    def s_arrived(f, dy, k):
        piece = held.at[shard(f, dy, other), span(k)]
        remote(piece, piece, ss.at[f, dy, k], sr.at[f, dy, k], sibling).wait_recv()

    def z1_copy(k):
        return remote(tok.at[span(k)], relay.at[k], z1s.at[k], z1r.at[k], zring[0 if k < 2 else 1])

    def z2_copy(k):
        way = 0 if k < 2 else 1
        oz = lax.rem(z + (6 if way == 0 else 2), 8)
        p = lax.div(oz, 4) * 8 + y * 2 + c
        return remote(relay.at[k], held.at[p, span(k)], z2s.at[k], z2r.at[k], zring[way])

    def take_y(f, way, j):
        y_arrived(f, way, j)
        if j < 4:
            if j in HALVES[way]:
                go(y_copy(f, way, 4 + HALVES[way].index(j)))
            go(s_copy(f, 3 if way == CW else 1, j))
        else:
            go(s_copy(f, 2, HALVES[way][j - 4]))

    def relay_on(k):
        remote(relay.at[k], relay.at[k], z1s.at[k], z1r.at[k], sibling).wait_recv()
        go(z2_copy(k))

    def take_z(k):
        piece = held.at[shard(1, 0, c), span(k)]
        remote(piece, piece, z2s.at[k], z2r.at[k], sibling).wait_recv()
        go(y_copy(1, CW, k))
        go(y_copy(1, CCW, k))
        go(s_copy(1, 0, k))

    def project(j):
        f, dy, cc = logical(j)
        if ORDER[j % 8][1]:
            for k in range(PIECES):
                s_arrived(f, dy, k)
        t = held[shard(f, dy, cc)]
        low = lax.dot_general(t, down[...], (((1,), (1,)), ((), ())), preferred_element_type=jnp.float32)
        acc = jnp.dot(t, w[...], preferred_element_type=jnp.float32)
        acc = acc + jnp.dot(low.astype(jnp.bfloat16), up[...], preferred_element_type=jnp.float32)
        acc = acc + bias[...].astype(jnp.float32)
        here = slice(j * rows, (j + 1) * rows)
        q[here, :HEAD] = (acc[:, :HEAD] * QSCALE).astype(jnp.bfloat16)
        column = lax.broadcasted_iota(jnp.int32, (rows, HEAD), 1)
        q[here, HEAD:] = jnp.where(column == j, 1.0, 0.0).astype(jnp.bfloat16)
        kv[here, :] = acc[:, HEAD:].astype(jnp.bfloat16)
        kt[:HEAD, here] = acc[:, HEAD:2 * HEAD].T.astype(jnp.bfloat16)
        va[here, :HEAD] = acc[:, 2 * HEAD:].astype(jnp.bfloat16)

    def size(ch):
        return SIZES[ch] * quarter

    def piece_rows(ch, n):
        return pl.ds(pl.multiple_of(STARTS[ch] * rows + n * size(ch), quarter), size(ch))

    def first(ch):
        return pl.ds(0, size(ch))

    def x1_copy(ch, d):
        return remote(kv.at[piece_rows(ch, lax.rem(x + d, 4))], xin.at[ch, x, first(ch)],
                      x1s.at[ch, d], x1r.at[ch, 4 - d], xs[d])

    def x2_copy(ch, d):
        return remote(xout.at[ch, d, first(ch)], refkv.at[piece_rows(ch, x)],
                      x2s.at[ch, d], x2r.at[ch, 4 - d], xs[d])

    def r_copy(ch):
        return remote(rs.at[ch, :, first(ch)], rr.at[ch, :, first(ch)], rsend.at[ch], rrecv.at[ch], right)

    def l_copy(ch):
        return remote(ls.at[ch, :, first(ch)], lr.at[ch, :, first(ch)], lsend.at[ch], lrecv.at[ch], left)

    columns = [lax.div(references[n], 4) for n in range(4)]
    planes = [lax.rem(references[n], 4) for n in range(4)]
    slots = [pairing[lax.rem(x + d, 4) * 4 + zl] for d in range(4)]

    def keys_send(ch):
        for d in (2, 1, 3):
            go(x1_copy(ch, d))
        xin[ch, x, first(ch)] = kv[piece_rows(ch, x), :]

    def is_mine(slot):
        return planes[slot] == zl

    def flow(ch, copy, incoming, outgoing, source, sink):
        if source:
            piece = incoming.at[ch, :, first(ch)]
            if incoming is rr:
                remote(piece, piece, rsend.at[ch], rrecv.at[ch], left).wait_recv()
            else:
                remote(piece, piece, lsend.at[ch], lrecv.at[ch], right).wait_recv()
        if sink:
            for slot in range(4):
                value = chosen[ch, slot, first(ch)]
                if source:
                    value = jnp.where(is_mine(slot), value, incoming[ch, slot, first(ch)])
                outgoing[ch, slot, first(ch)] = value
            copy(ch).start()

    def keys_step(t):
        if t < CHUNKS:
            for d in (1, 3, 2):
                piece = xin.at[t, lax.rem(x + d, 4), first(t)]
                remote(piece, piece, x1s.at[t, d], x1r.at[t, d], xs[d]).wait_recv()
            here = [xin[t, n, first(t)] for n in range(4)]
            for slot in range(4):
                chosen[t, slot, first(t)] = pick(here, columns[slot])

        for line in range(4):
            rc, lc = t - LAG * line, t - LAG * (3 - line)

            @pl.when(zl == line)
            def _():
                def rightward():
                    if 0 <= rc < CHUNKS:
                        flow(rc, r_copy, rr, rs, line > 0, line < 3)

                def leftward():
                    if 0 <= lc < CHUNKS:
                        flow(lc, l_copy, lr, ls, line < 3, line > 0)

                if line < 2:
                    rightward()
                    leftward()
                else:
                    leftward()
                    rightward()

        ch = t - 3 * LAG
        if 0 <= ch < CHUNKS:
            final = []
            for slot in range(4):
                far = jnp.where(planes[slot] < zl, rr[ch, slot, first(ch)], lr[ch, slot, first(ch)])
                final.append(jnp.where(is_mine(slot), chosen[ch, slot, first(ch)], far))
            for d in (2, 1, 3):
                xout[ch, d, first(ch)] = pick(final, slots[d])
                go(x2_copy(ch, d))
            refkv[piece_rows(ch, x), :] = pick(final, slots[0])

    def keys_take(ch):
        for d in (1, 3, 2):
            piece = refkv.at[piece_rows(ch, lax.rem(x + d, 4))]
            remote(piece, piece, x2s.at[ch, d], x2r.at[ch, d], xs[d]).wait_recv()
        count = SIZES[ch] * rows
        got = refkv[STARTS[ch] * rows:STARTS[ch] * rows + count, :]
        base = (16 + STARTS[ch]) * rows
        kt[:HEAD, base:base + count] = got[:, :HEAD].astype(jnp.float32).T.astype(jnp.bfloat16)
        va[base:base + count, :HEAD] = got[:, HEAD:]

    def block(b):
        return slice(b * QROWS, (b + 1) * QROWS)

    def scores(b, keys, slot):
        k0, k1 = keys
        qt = q[block(b), :]
        top = None
        for k in range(k0, k1, KSTEP):
            score = jnp.dot(qt, kt[:, k:k + KSTEP], preferred_element_type=jnp.float32)
            s[slot, :, k - k0:k - k0 + KSTEP] = score
            for m in range(KSTEP // 128):
                piece = score[:, m * 128:(m + 1) * 128]
                top = piece if top is None else jnp.maximum(top, piece)
        return jnp.broadcast_to(jnp.max(top, axis=1, keepdims=True), (QROWS, 128))

    def mix(b, keys, slot, top, fresh):
        k0, k1 = keys
        acc = None
        if not fresh:
            old = top_all[block(b), :]
            top = jnp.maximum(top, old)
            shrink = jnp.exp2(old - top)
            acc = jnp.concatenate([acc_all[block(b), :HEAD] * shrink, acc_all[block(b), HEAD:] * shrink], axis=1)
        top_all[block(b), :] = top
        wide = jnp.concatenate([top] * (KSTEP // 128), axis=1)
        for k in range(k0, k1, KSTEP):
            weight = jnp.exp2((s[slot, :, k - k0:k - k0 + KSTEP] - wide).astype(jnp.bfloat16))
            more = jnp.dot(weight, va[k:k + KSTEP, :], preferred_element_type=jnp.float32)
            acc = more if acc is None else acc + more
        return acc

    def attend(blocks, keys, fresh=False, done=None):
        tops = [scores(blocks[0], keys, 0)]
        for n, b in enumerate(blocks):
            if n + 1 < len(blocks):
                tops.append(scores(blocks[n + 1], keys, (n + 1) % 2))
            acc = mix(b, keys, n % 2, tops[n], fresh)
            if done is None:
                acc_all[block(b), :] = acc
            else:
                done(b, acc)

    def my_columns():
        return pl.ds(pl.multiple_of(me * HEAD, HEAD), HEAD)

    def o_copy(j):
        place_there = (j // 8) * 8 + MIRROR[j % 8]
        return remote(mixed.at[j], out.at[:, my_columns()], os.at[j], orv.at[place_there], owners[j])

    def finish(b, acc):
        result = (acc[:, :HEAD] / acc[:, HEAD:HEAD + 1]).astype(jnp.bfloat16)
        for n in range(QROWS // TILE):
            j = b * (QROWS // TILE) + n
            if j == 0:
                out[:, my_columns()] = result[:TILE]
            else:
                mixed[j] = result[n * TILE:(n + 1) * TILE]
                go(o_copy(j))

    local[0].wait()
    for k in (0, 2, 1, 3):
        go(z1_copy(k))
    for j in range(4):
        go(y_copy(0, CW, j))
        go(y_copy(0, CCW, (2, 3, 0, 1)[j]))
    for k in range(PIECES):
        go(s_copy(0, 0, k))

    tiles = mask.shape[0]
    tile_row = lax.broadcasted_iota(jnp.int32, (tiles, 2 * tiles), 0)
    tile_col = lax.broadcasted_iota(jnp.int32, (tiles, 2 * tiles), 1)
    allow = jnp.where((mask[...] == 1) | (tile_row == tile_col), 1.0, 0.0).astype(jnp.bfloat16)

    def order_of(tile):
        far = jnp.where(lax.div(tile, 8) == zh, 0, 8)
        dy = lax.rem(lax.rem(lax.div(tile, 2), 4) + 4 - y, 4)
        o = jnp.where(lax.rem(tile, 2) == c, 0, 1)
        near = jnp.where(dy == 0, o, jnp.where(dy == 2, 6 + o, jnp.where(dy == 3, 2, 3) + 2 * o))
        return far + near

    turn = jnp.where(
        order_of(lax.broadcasted_iota(jnp.int32, (tiles, tiles), 1)) == lax.broadcasted_iota(jnp.int32, (tiles, tiles), 0),
        1.0, 0.0).astype(jnp.bfloat16)
    turned = jnp.dot(turn, allow, preferred_element_type=jnp.float32).astype(jnp.bfloat16)
    spread_shape = (tiles, tiles * TILE)
    spread = jnp.where(
        order_of(lax.broadcasted_iota(jnp.int32, spread_shape, 0)) == lax.div(lax.broadcasted_iota(jnp.int32, spread_shape, 1), TILE),
        1.0, 0.0).astype(jnp.bfloat16)
    for side in range(2):
        wide = jnp.dot(turned[:, side * tiles:(side + 1) * tiles], spread, preferred_element_type=jnp.float32)
        kt[HEAD:HEAD + tiles, side * tiles * TILE:(side + 1) * tiles * TILE] = jnp.where(wide > 0.5, 0.0, LOW).astype(jnp.bfloat16)
    kt[HEAD + tiles:, :] = jnp.zeros((HEAD - tiles, 2 * tiles * TILE), jnp.bfloat16)
    va[:, HEAD:] = jnp.ones((2 * tiles * TILE, HEAD), jnp.bfloat16)

    for copy in local[1:]:
        copy.wait()
    project(0)
    take_y(0, CW, 0)
    take_y(0, CCW, 2)
    project(1)
    keys_send(0)
    relay_on(0)
    relay_on(2)
    take_y(0, CW, 1)
    take_y(0, CCW, 3)
    take_y(0, CW, 2)
    take_y(0, CCW, 0)
    relay_on(1)
    relay_on(3)
    take_y(0, CW, 3)
    take_y(0, CCW, 1)
    project(2)
    project(3)
    keys_send(1)
    take_z(0)
    take_z(2)
    keys_step(0)
    project(4)
    project(5)
    keys_send(2)
    take_y(0, CW, 4)
    take_y(0, CCW, 4)
    take_y(0, CW, 5)
    take_y(0, CCW, 5)
    take_y(1, CW, 0)
    take_y(1, CCW, 2)
    keys_step(1)
    project(6)
    take_z(1)
    take_z(3)
    keys_step(2)
    project(8)
    take_y(1, CW, 2)
    take_y(1, CCW, 0)
    project(7)
    keys_send(3)
    project(9)
    keys_send(4)
    keys_step(3)
    take_y(1, CW, 1)
    take_y(1, CCW, 3)
    keys_step(4)
    attend((0, 1), OWN0, True)
    take_y(1, CW, 4)
    take_y(1, CCW, 4)
    take_y(1, CW, 3)
    take_y(1, CCW, 1)
    project(10)
    project(11)
    keys_send(5)
    take_y(1, CW, 5)
    take_y(1, CCW, 5)
    keys_step(5)
    project(12)
    keys_send(6)
    project(13)
    keys_send(7)
    keys_step(6)
    project(14)
    keys_send(8)
    keys_step(7)
    project(15)
    keys_send(9)
    keys_step(8)
    attend((2, 3), OWN0, True)
    keys_step(9)
    keys_step(10)
    attend((0, 1), OWN1)
    keys_step(11)
    keys_step(12)
    attend((2, 3), OWN1)
    keys_step(13)
    for ch in range(4):
        keys_take(ch)
    attend((0, 1), REF0)
    keys_step(14)
    attend((2, 3), REF0)
    keys_step(15)
    for ch in (4, 5, 6, 7):
        keys_take(ch)
    attend((0, 1, 2, 3), REF1)
    for ch in (8, 9):
        keys_take(ch)
    attend((2, 3, 0, 1), LAST, done=finish)
    for copy in started:
        copy.wait_send()

    @pl.when(zl < 3)
    def _():
        for ch in range(CHUNKS):
            r_copy(ch).wait_send()

    @pl.when(zl > 0)
    def _():
        for ch in range(CHUNKS):
            l_copy(ch).wait_send()

    for j in range(1, 16):
        f, dy, cc = logical(j)
        there = out.at[:, pl.ds(pl.multiple_of(shard(f, dy, cc) * HEAD, HEAD), HEAD)]
        remote(there, there, os.at[j], orv.at[j], owners[j]).wait_recv()


def whole_block(references, pairing, mask, bias, tok, w, down, up):
    rows, width = tok.shape
    length = 16 * rows
    dma = pltpu.SemaphoreType.DMA
    vmem = pl.BlockSpec(memory_space=pltpu.VMEM)
    smem = pl.BlockSpec(memory_space=pltpu.SMEM)
    anywhere = pl.BlockSpec(memory_space=pl.ANY)
    half = jnp.bfloat16
    pieces = pltpu.VMEM((CHUNKS, 4, rows // 2, 2 * HEAD), half)
    return pl.pallas_call(
        block_kernel,
        out_shape=jax.ShapeDtypeStruct((rows, 16 * HEAD), half),
        in_specs=[smem, smem, vmem, vmem] + [anywhere] * 4,
        out_specs=vmem,
        scratch_shapes=[
            pltpu.VMEM((16, rows, width), half),
            pltpu.VMEM((PIECES, rows // PIECES, width), half),
            pltpu.VMEM(w.shape, half),
            pltpu.VMEM(down.shape, half),
            pltpu.VMEM(up.shape, half),
            pltpu.VMEM((length, 2 * HEAD), half),
            pltpu.VMEM((2 * HEAD, 2 * length), half),
            pltpu.VMEM((2 * length, 2 * HEAD), half),
            pltpu.VMEM((length, 2 * HEAD), half),
            pltpu.VMEM((length, 2 * HEAD), half),
            pieces, pieces, pieces, pieces, pieces, pieces, pieces,
            pltpu.VMEM((2, QROWS, KROWS), jnp.float32),
            pltpu.VMEM((length, 128), jnp.float32),
            pltpu.VMEM((length, 2 * HEAD), jnp.float32),
            pltpu.VMEM((16, rows, HEAD), half),
            dma((4,)),
            dma((4,)), dma((4,)), dma((4,)), dma((4,)),
            dma((2, 2, 6)), dma((2, 2, 6)),
            dma((2, 4, 4)), dma((2, 4, 4)),
            dma((CHUNKS, 4)), dma((CHUNKS, 4)),
            dma((CHUNKS,)), dma((CHUNKS,)), dma((CHUNKS,)), dma((CHUNKS,)),
            dma((CHUNKS, 4)), dma((CHUNKS, 4)),
            dma((16,)), dma((16,)),
        ],
        compiler_params=pltpu.CompilerParams(
            collective_id=0, has_side_effects=True, vmem_limit_bytes=56 * 2**20),
        name="attention_block",
    )(references, pairing, mask, bias, tok, w, down, up)


def on_device(tokens, projection_weight, projection_bias, adapter_down_weight, adapter_up_weight,
              tile_allow_mask, references, pairing):
    return whole_block(references, pairing, tile_allow_mask[0], projection_bias, tokens[0],
                       projection_weight[:, 0], adapter_down_weight[0].T, adapter_up_weight[0, :, 0])[None]


def solution(mesh):
    in_specs = (
        P("req", "patch", None),
        P(None, "patch", None),
        P("patch", None),
        P("req", None, None),
        P("req", None, "patch", None),
        P("req", None, None),
        P(),
        P(),
    )
    return jax.shard_map(
        on_device, mesh=mesh, in_specs=in_specs, out_specs=P("req", "patch", None), check_vma=False
    )
```
